256 devices in a mesh: replica: 16 (over x, y_hi, core), tensor: 16 (over z, y_lo).
Axes of the slice: x: 4, y: 4 (y_hi: 2, y_lo: 2; y = y_hi * 2 + y_lo), z: 8, core: 2. Of those that a mesh axis runs over, the one named last changes fastest.
Arguments:
- queries: bfloat16 [16, 512, 10240], P('replica', None, 'tensor'), may hold values from -160 to 160
- key_rows: bfloat16 [16, 512, 10240], P('replica', None, 'tensor'), may hold values from -4 to 4
- value_rows: bfloat16 [16, 512, 10240], P('replica', None, 'tensor'), may hold values from -6 to 6
- out_grads: bfloat16 [16, 512, 1024], P('replica', 'tensor'), may hold values from -6 to 6
- inner_weights: bfloat16 [16, 80, 128, 1024], P('replica', 'tensor'), may hold values from -0.078125 to 0.078125
- adam_first: bfloat16 [16, 80, 128, 1024], P('replica', 'tensor'), may hold values from -12 to 12
- adam_second: bfloat16 [16, 80, 128, 1024], P('replica', 'tensor'), may hold values from 1 to 16
- anchor: bfloat16 [80, 128, 1024], P('tensor'), may hold values from -0.0625 to 0.0625
- momentum: float32 [80, 128, 1024], P('tensor', 'replica'), may hold values from -0.06 to 0.06
Outputs:
- query_grads: bfloat16 [16, 512, 10240], P('replica', None, 'tensor')
- key_grads: bfloat16 [16, 512, 10240], P('replica', None, 'tensor')
- value_grads: bfloat16 [16, 512, 10240], P('replica', None, 'tensor')
- new_first: bfloat16 [16, 80, 128, 1024], P('replica', 'tensor')
- new_second: bfloat16 [16, 80, 128, 1024], P('replica', 'tensor')
- new_anchor: bfloat16 [80, 128, 1024], P('tensor')
- new_momentum: float32 [80, 128, 1024], P('tensor', 'replica')
The draws below stay inside these ranges and needn't reach their ends.
All inputs are finite; a program needn't handle non-finite values.
Results may differ from the reference program's by a relative error of at most 0.028.
Values may be sent and summed in bfloat16 or wider, within the bound.
No kernel may reach another device: no remote copies, remote signals or barrier semaphores. Data moves between devices by JAX's collectives and lax.ppermute only.
A program may use at most 64 MiB of HBM per device.

```python
import math
import jax
import jax.numpy as jnp
from jax import lax

D = 1024
DH = 128
LEN = 512
WORKERS = 16
HEADS = 80
INNER = 10240


def drawn_pair(key):
    base = jax.random.fold_in(key, 11)
    query_key, row_key = jax.random.split(base, 2)
    shape = (WORKERS, HEADS, LEN, DH)
    query_heads = jnp.clip(jax.random.normal(query_key, shape, jnp.float32), -6.0, 6.0)
    key_heads = jnp.clip(jax.random.normal(row_key, shape, jnp.float32), -4.0, 4.0)
    return (query_heads, key_heads)


def widened(head_array):
    return jnp.transpose(head_array, (0, 2, 1, 3)).reshape(WORKERS, LEN, HEADS * DH).astype(jnp.bfloat16)


def draw_queries(key, part):
    return widened(drawn_pair(key)[0])


def draw_key_rows(key, part):
    return widened(drawn_pair(key)[1])


def strengthened(entries, stream_key, source, target, blocks, factor):
    def block_of(dim):
        return (jnp.arange(entries.shape[dim]) // (entries.shape[dim] // blocks)).reshape((-1,) + (1,) * (entries.ndim - 1 - dim))

    first = jax.random.permutation(stream_key, blocks)[block_of(target)]
    second = (block_of(target) + blocks // 2) % blocks
    return jnp.where((block_of(source) == first) | (block_of(source) == second), factor * entries, entries)


def levels(own_key, dims, shards, smallest, top_value):
    def one(axis_at, blocks):
        steps = jax.random.uniform(jax.random.fold_in(jax.random.fold_in(own_key, 6), axis_at), (blocks,), jnp.float32, smallest / len(shards), top_value / len(shards))
        return jnp.repeat(jnp.exp(steps), dims[axis_at] // blocks).reshape((-1,) + (1,) * (len(dims) - axis_at - 1))

    factor_of = one(*shards[0])
    for cut in shards[1:]:
        factor_of = factor_of * one(*cut)
    return factor_of


def gaussian(key, shape, scale, reach, cuts=(), held_as=jnp.bfloat16):
    drawn = jax.random.normal(key, shape, jnp.float32) * scale
    if len(cuts) > 0:
        drawn = levels(key, shape, cuts, -0.22, 0.18) * drawn
    return jnp.clip(drawn, min=-reach, max=reach).astype(held_as)


def bell_draw_with(rng, extent, deviation, limit, cuts, heavy, held_as=jnp.bfloat16):
    values = deviation * jax.random.normal(rng, extent, jnp.float32)
    if cuts:
        values = values * levels(rng, extent, cuts, -0.22, 0.18)
    return jnp.clip(strengthened(values, jax.random.fold_in(rng, 3), *heavy), -limit, limit).astype(held_as)


def setup_inputs(seed: int = 0) -> dict:
    key_list = jax.random.split(jax.random.key(seed), 10)
    queries = draw_queries(jax.random.fold_in(key_list[9], 71), 0)
    key_rows = draw_key_rows(jax.random.fold_in(key_list[9], 71), 0)
    value_rows = gaussian(key_list[2], (WORKERS, LEN, INNER), 1.0, 6.0, ((0, 16), (2, 16)))
    out_grads = gaussian(key_list[3], (WORKERS, LEN, D), 1.0, 6.0, ((0, 16), (1, 16)))
    inner_weights = bell_draw_with(key_list[4], (WORKERS, HEADS, DH, D), INNER ** -0.5, 0.078125, ((0, 16), (1, 16)), (0, 2, 16, 2.0))
    adam_first = gaussian(key_list[5], (WORKERS, HEADS, DH, D), 2.0, 12.0, ((0, 16), (1, 16)))
    adam_second = jnp.clip(jnp.exp(math.log(16.0) - 2.7725887 * jax.random.uniform(key_list[6], (WORKERS, HEADS, DH, D), jnp.float32) ** levels(key_list[6], (WORKERS, HEADS, DH, D), ((0, 16), (1, 16)), -0.2, 0.2)), 1.0, 16.0).astype(jnp.bfloat16)
    anchor = gaussian(key_list[7], (HEADS, DH, D), INNER ** -0.5, 0.0625, ((0, 16),))
    momentum = gaussian(key_list[8], (HEADS, DH, D), 0.01, 0.06, ((0, 16), (1, 16)), jnp.float32)
    return dict(queries=queries, key_rows=key_rows, value_rows=value_rows, out_grads=out_grads, inner_weights=inner_weights, adam_first=adam_first, adam_second=adam_second, anchor=anchor, momentum=momentum)


beta_first = 0.9
beta_second = 0.95
correct_first = 0.9999734386011124
correct_second = 0.994079470779666
inner_rate = 0.01
decay_rate = 0.1
epsilon = 1e-08
outer_rate = 0.7
outer_beta = 0.9
highest = lax.Precision.HIGHEST

def lowered(values):
    return lax.optimization_barrier(values.astype(jnp.bfloat16)).astype(jnp.float32)

def worker_step(queries, key_rows, value_rows, out_grads, inner_weights, adam_first, adam_second, anchor_wide):
    score_scale = 1.0 / math.sqrt(DH)
    query_heads = queries.astype(jnp.float32).reshape(LEN, HEADS, DH)
    key_heads = key_rows.astype(jnp.float32).reshape(LEN, HEADS, DH)
    value_heads = value_rows.astype(jnp.float32).reshape(LEN, HEADS, DH)
    grads_out = out_grads.astype(jnp.float32)
    previous = inner_weights.astype(jnp.float32)
    scores = jnp.einsum('qhc,khc->hqk', query_heads, key_heads, precision=highest) * score_scale
    probs = jax.nn.softmax(scores, axis=-1)
    probs_low = lowered(probs)
    attention = lowered(jnp.einsum('hqk,khc->qhc', probs_low, value_heads, precision=highest))
    grad_proj = jnp.einsum('qhc,qd->hcd', attention, grads_out, precision=highest)
    grad_attn = lowered(jnp.einsum('qd,hcd->qhc', grads_out, previous, precision=highest))
    value_grads = jnp.einsum('hqk,qhc->khc', probs_low, grad_attn, precision=highest).astype(jnp.bfloat16)
    grad_probs = jnp.einsum('qhc,khc->hqk', grad_attn, value_heads, precision=highest)
    row_dot = jnp.einsum('qhc,qhc->hq', grad_attn, attention, precision=highest)
    grad_scores = lowered(probs * (grad_probs - row_dot[:, :, None]))
    query_grads = (jnp.einsum('hqk,khc->qhc', grad_scores, key_heads, precision=highest) * score_scale).astype(jnp.bfloat16)
    key_grads = (jnp.einsum('hqk,qhc->khc', grad_scores, query_heads, precision=highest) * score_scale).astype(jnp.bfloat16)
    first_moment = beta_first * adam_first.astype(jnp.float32) + (1.0 - beta_first) * grad_proj
    second_moment = beta_second * adam_second.astype(jnp.float32) + (1.0 - beta_second) * grad_proj * grad_proj
    stepped = previous - inner_rate * (first_moment / correct_first / (jnp.sqrt(second_moment / correct_second) + epsilon) + decay_rate * previous)
    delta_terms = (anchor_wide - stepped).astype(jnp.bfloat16)
    return (query_grads.reshape(LEN, INNER), key_grads.reshape(LEN, INNER), value_grads.reshape(LEN, INNER), first_moment.astype(jnp.bfloat16), second_moment.astype(jnp.bfloat16), delta_terms)

def reference(queries, key_rows, value_rows, out_grads, inner_weights, adam_first, adam_second, anchor, momentum):
    anchor_wide = anchor.astype(jnp.float32)

    def visit(summed, inputs):
        results = worker_step(*inputs, anchor_wide)
        deltas = lax.optimization_barrier(results[5]).astype(jnp.float32)
        return (summed + deltas, results[:5])
    summed, stacked = lax.scan(visit, jnp.zeros((HEADS, DH, D), jnp.float32), (queries, key_rows, value_rows, out_grads, inner_weights, adam_first, adam_second))
    average = summed / WORKERS
    new_momentum = outer_beta * momentum + average
    new_anchor = (anchor_wide - outer_rate * (average + outer_beta * new_momentum)).astype(jnp.bfloat16)
    return (stacked[0], stacked[1], stacked[2], stacked[3], stacked[4], new_anchor, new_momentum)
```

```python
import functools
import math

import jax
import jax.numpy as jnp
from jax import lax
from jax.experimental import pallas as pl
from jax.experimental.pallas import tpu as pltpu
from jax.sharding import PartitionSpec as P

DH = 128
HALF = 512

beta_first = 0.9
beta_second = 0.95
correct_first = 0.9999734386011124
correct_second = 0.994079470779666
inner_rate = 0.01
decay_rate = 0.1
epsilon = 1e-08
outer_rate = 0.7
outer_beta = 0.9
workers = 16
score_scale = 1.0 / math.sqrt(DH)

NT = (((1,), (1,)), ((), ()))
TN = (((0,), (0,)), ((), ()))
f32, bf16 = jnp.float32, jnp.bfloat16
WHOLE = pl.BlockSpec(memory_space=pltpu.VMEM)
SCALARS = pl.BlockSpec(memory_space=pltpu.SMEM)
MIB = 1024 * 1024


def dot(a, b, dims=(((1,), (0,)), ((), ()))):
    return lax.dot_general(a, b, dims, preferred_element_type=f32)


def call(kernel, name, args, outs, scratch=(), mib=8, flops=0, exps=0):
    moved = sum(a.size * a.dtype.itemsize for a in args) + sum(
        math.prod(o.shape) * jnp.dtype(o.dtype).itemsize for o in outs
    )
    return pl.pallas_call(
        kernel,
        in_specs=[SCALARS if a.dtype == jnp.int32 else WHOLE for a in args],
        out_specs=[WHOLE] * len(outs),
        out_shape=outs,
        scratch_shapes=list(scratch),
        compiler_params=pltpu.CompilerParams(vmem_limit_bytes=mib * MIB),
        cost_estimate=pl.CostEstimate(flops=flops, bytes_accessed=moved, transcendentals=exps),
        name=name,
    )(*args)


def near(shape, dtype=bf16):
    return pltpu.VMEM(shape, dtype)


def far(shape, dtype=bf16):
    return jax.ShapeDtypeStruct(shape, dtype)


def columns_of(h):
    return slice(h * DH, (h + 1) * DH)


def forward_kernel(heads, q_ref, k_ref, v_ref, att_ref, p_ref):
    for h in range(heads):
        at = columns_of(h)
        s = dot(k_ref[:, at], q_ref[:, at], NT)
        top = jnp.max(s, axis=0, keepdims=True)
        e = jnp.exp((s - top) * score_scale)
        total = jnp.sum(e, axis=0, keepdims=True)
        p = (e * (1.0 / total)).astype(bf16)
        p_ref[h] = p
        att_ref[h] = dot(v_ref[:, at], p, TN).astype(bf16)


def forward(q, k, v):
    length, width = q.shape
    heads = width // DH
    return call(
        functools.partial(forward_kernel, heads),
        "attention_forward",
        [q, k, v],
        [near((heads, DH, length)), near((heads, length, length))],
        flops=4 * heads * length * length * DH,
        exps=heads * length * length,
    )


PIECES = ((0, 0, 1), (0, 1, 1), (2, 0, 2), (-2, 0, 2), (1, 0, 2), (-1, 0, 2), (4, 0, 1), (4, 1, 1), (3, 0, 2), (-3, 0, 2))


def in_order(z, low, pieces, rows_ref):
    for ref, (ahead, first, lanes) in zip(pieces, PIECES):
        for n in range(lanes):
            lane = low if first + n == 0 else 1 - low
            start = (((z + 8 + ahead) % 8) * 2 + lane) * 32
            rows_ref[pl.ds(pl.multiple_of(start, 32), 32), :] = ref[n * 32 : n * 32 + 32, :]


CHUNK = 16


def moments(g, m, v):
    first = beta_first * m.astype(f32) + (1.0 - beta_first) * g
    second = beta_second * v.astype(f32) + (1.0 - beta_second) * g * g
    return first, second


def delta_kernel(ordered, side, sc, *refs):
    if ordered:
        rows_ref, refs = refs[0], refs[1:]
    else:
        pieces, refs = refs[:10], refs[10:]
        rows_ref = refs[-2]
        in_order(sc[1], sc[2], pieces, rows_ref)
    att_ref, w_ref, m_ref, v_ref, a_ref, d_ref = refs[:6]
    g_ref = refs[-1]
    half = sc[0] if side else 1 - sc[0]
    cols = pl.ds(pl.multiple_of(half * HALF, HALF), HALF)
    for h in range(att_ref.shape[0]):
        g_ref[...] = dot(att_ref[h], rows_ref[:, cols])

        def chunk(i, carry):
            at = pl.ds(pl.multiple_of(i * CHUNK, CHUNK), CHUNK)
            first, second = moments(g_ref[at, :], m_ref[h, at, cols], v_ref[h, at, cols])
            t = second * (1.0 / correct_second)
            root = jnp.sqrt(t) + epsilon
            moved = (inner_rate / correct_first) * first / root
            kept = (1.0 - inner_rate * decay_rate) * w_ref[h, at, cols].astype(f32)
            d_ref[h, at, :] = (a_ref[h, at, cols].astype(f32) - kept + moved).astype(bf16)
            return carry

        lax.fori_loop(0, DH // CHUNK, chunk, 0, unroll=True)


def delta(side, sc, rows, att, w, m, v, anchor):
    heads, _, length = att.shape
    wide = w.shape[2]
    ordered = not isinstance(rows, list)
    outs = [near((heads, DH, HALF))]
    if not ordered:
        outs.append(near((length, wide)))
    return call(
        functools.partial(delta_kernel, ordered, side),
        "delta_" + ("own" if side else "other"),
        [sc] + ([rows] if ordered else rows) + [att, w, m, v, anchor],
        outs,
        [pltpu.VMEM((DH, HALF), f32)],
        flops=2 * heads * DH * length * HALF,
        exps=2 * heads * DH * HALF,
    )


def moments_kernel(rows_ref, att_ref, m_ref, v_ref, mo_ref, vo_ref, g_ref):
    for h in range(att_ref.shape[0]):
        g_ref[...] = dot(att_ref[h], rows_ref[...])

        def chunk(i, carry):
            at = pl.ds(pl.multiple_of(i * CHUNK, CHUNK), CHUNK)
            first, second = moments(g_ref[at, :], m_ref[h, at, :], v_ref[h, at, :])
            mo_ref[h, at, :] = first.astype(bf16)
            vo_ref[h, at, :] = second.astype(bf16)
            return carry

        lax.fori_loop(0, DH // CHUNK, chunk, 0, unroll=True)


def new_moments(rows, att, m, v):
    heads, _, length = att.shape
    wide = rows.shape[1]
    return call(
        moments_kernel,
        "moments",
        [rows, att, m, v],
        [far(m.shape), far(v.shape)],
        [pltpu.VMEM((DH, wide), f32)],
        flops=2 * heads * DH * length * wide,
    )


def backward_kernel(rows_ref, w_ref, q_ref, k_ref, v_ref, att_ref, p_ref, qg_ref, kg_ref, vg_ref):
    for h in range(att_ref.shape[0]):
        at = columns_of(h)
        grads = dot(rows_ref[...], w_ref[h], NT).astype(bf16)
        p = p_ref[h]
        turned = jnp.transpose(grads.astype(f32))
        row_dot = jnp.sum(turned * att_ref[h].astype(f32), axis=0, keepdims=True)
        vg_ref[:, at] = dot(p, grads).astype(bf16)
        grad_probs = dot(v_ref[:, at], grads, NT)
        grad_scores = (p.astype(f32) * (grad_probs - row_dot)).astype(bf16)
        kg_ref[:, at] = (dot(grad_scores, q_ref[:, at]) * score_scale).astype(bf16)
        qg = dot(k_ref[:, at], grad_scores, TN) * score_scale
        qg_ref[:, at] = jnp.transpose(qg).astype(bf16)


def backward(rows, w, q, k, v, att, p):
    length, width = q.shape
    wide = rows.shape[1]
    return call(
        backward_kernel,
        "attention_backward",
        [rows, w, q, k, v, att, p],
        [far((length, width))] * 3,
        flops=2 * length * width * wide + 8 * width * length * length,
    )


def half_of(index):
    return pl.ds(pl.multiple_of(index * HALF, HALF), HALF)


def slot_of(index):
    return pl.ds(pl.multiple_of(index * 32, 32), 32)


def pair_kernel(a_ref, b_ref, o_ref):
    o_ref[:32, :] = a_ref[...]
    o_ref[32:, :] = b_ref[...]


def pair_of(own, other):
    rows, wide = own.shape
    return call(pair_kernel, "row_pair", [own, other], [near((2 * rows, wide))], mib=2)[0]


def share_kernel(sc, m_ref, mine_ref, theirs_ref):
    mine_ref[...] = m_ref[:, :, half_of(sc[0])]
    theirs_ref[...] = m_ref[:, :, half_of(1 - sc[0])]


def momentum_shares(sc, momentum):
    heads, rows, _ = momentum.shape
    shape = (heads, rows, HALF)
    return call(share_kernel, "momentum_shares", [sc, momentum], [near(shape, f32)] * 2, mib=2)


def stack_kernel(sc, mine_ref, came_ref, o_ref):
    o_ref[:, pl.ds(pl.multiple_of(sc[0] * 8, 8), 8), :] = mine_ref[...]
    o_ref[:, pl.ds(pl.multiple_of((1 - sc[0]) * 8, 8), 8), :] = came_ref[...]


def momentum_stack(sc, mine, came):
    heads, rows, _ = mine.shape
    return call(stack_kernel, "momentum_stack", [sc, mine, came], [near((heads, 2 * rows, HALF), f32)], mib=2)[0]


HOPS = (1, 3, 2)


def chip_kernel(sc, a_ref, b_ref, *outs):
    for out, hop in zip(outs, (0,) + HOPS):
        at = slot_of(sc[3] ^ hop)
        out[...] = (a_ref[:, at, :].astype(f32) + b_ref[:, at, :].astype(f32)).astype(bf16)


def chip_sum(sc, own, came):
    heads = own.shape[0]
    return call(chip_kernel, "chip_sum", [sc, own, came], [near((heads, 32, HALF))] * 4, mib=2)


def line_kernel(a_ref, b_ref, c_ref, d_ref, o_ref):
    total = a_ref[...].astype(f32) + b_ref[...].astype(f32)
    o_ref[...] = (total + c_ref[...].astype(f32) + d_ref[...].astype(f32)).astype(bf16)


def line_sum(parts):
    return call(line_kernel, "line_sum", list(parts), [near(parts[0].shape)], mib=2)[0]


def outer_kernel(sc, p_ref, q_ref, a_ref, near_ref, far_ref, new_ref, kept_ref, sent_ref, mom_ref):
    y = sc[4]
    mom_ref[:, pl.ds(pl.multiple_of(y * 16, 16), 16), :] = near_ref[...]
    mom_ref[:, pl.ds(pl.multiple_of((1 - y) * 16, 16), 16), :] = far_ref[...]
    average = (p_ref[...].astype(f32) + q_ref[...].astype(f32)) * (1.0 / workers)
    momentum = outer_beta * mom_ref[...] + average
    anchor = a_ref[:, slot_of(sc[3]), half_of(sc[0])].astype(f32)
    new_ref[...] = (anchor - outer_rate * (average + outer_beta * momentum)).astype(bf16)
    mom_ref[...] = momentum
    kept_ref[...] = mom_ref[:, pl.ds(pl.multiple_of(y * 16 + sc[0] * 8, 8), 8), :]
    sent_ref[...] = mom_ref[:, pl.ds(pl.multiple_of(y * 16 + (1 - sc[0]) * 8, 8), 8), :]


def outer(sc, p, q, anchor, momentum, across):
    heads = p.shape[0]
    row = (heads, 8, HALF)
    return call(
        outer_kernel,
        "outer_step",
        [sc, p, q, anchor, momentum, across],
        [near(p.shape), near(row, f32), near(row, f32)],
        [pltpu.VMEM(p.shape, f32)],
        mib=4,
    )


def place_kernel(sc, *refs):
    for ref, hop in zip(refs[:4], (0,) + HOPS):
        refs[4][:, slot_of(sc[3] ^ hop), :] = ref[...]


def placed(sc, parts):
    heads = parts[0].shape[0]
    return call(place_kernel, "place_slots", [sc] + list(parts), [near((heads, 128, HALF))], mib=2)[0]


def join_kernel(sc, mine_ref, came_ref, o_ref):
    o_ref[:, :, half_of(sc[0])] = mine_ref[...]
    o_ref[:, :, half_of(1 - sc[0])] = came_ref[...]


def joined(sc, mine, came, name):
    heads, rows, _ = mine.shape
    return call(join_kernel, name, [sc, mine, came], [far((heads, rows, 2 * HALF), mine.dtype)], mib=2)[0]


def swapped(value, axis, bit):
    return lax.ppermute(value, axis, [(i, i ^ bit) for i in range(16)])


def from_ahead(value, k):
    return lax.ppermute(
        value, "tensor", [(i, ((i // 2 - k) % 8) * 2 + i % 2) for i in range(16)]
    )


def gather_rows(pair, own, other):
    b2 = from_ahead(pair, 2)
    m2 = from_ahead(pair, -2)
    b1 = from_ahead(pair, 1)
    m1 = from_ahead(pair, -1)
    b4 = from_ahead(b2[:32], 2)
    m4 = from_ahead(m2[32:], -2)
    b3 = from_ahead(b2, 1)
    m3 = from_ahead(m2, -1)
    return [own, other, b2, m2, b1, m1, b4, m4, b3, m3]


def local(queries, key_rows, value_rows, out_grads, inner_weights, adam_first, adam_second, anchor, momentum):
    replica, tensor = lax.axis_index("replica"), lax.axis_index("tensor")
    sc = jnp.stack([replica & 1, tensor >> 1, tensor & 1, replica >> 2, (replica >> 1) & 1]).astype(jnp.int32)
    own, q, k, v, sc = lax.optimization_barrier((out_grads[0], queries[0], key_rows[0], value_rows[0], sc))
    w, m, s = inner_weights[0], adam_first[0], adam_second[0]

    other = swapped(own, "tensor", 1)
    att, probs = forward(q, k, v)
    other, att, probs = lax.optimization_barrier((other, att, probs))
    pieces = gather_rows(pair_of(own, other), own, other)

    mine, theirs = momentum_shares(sc, momentum)
    slot_momentum = momentum_stack(sc, mine, swapped(theirs, "replica", 1))
    far_momentum = swapped(slot_momentum, "replica", 2)

    d_other, rows = delta(0, sc, pieces, att, w, m, s, anchor)
    came = swapped(d_other, "replica", 1)
    (d_own,) = delta(1, sc, rows, att, w, m, s, anchor)
    parts = chip_sum(sc, d_own, came)
    arrived = [swapped(part, "replica", 4 * hop) for part, hop in zip(parts[1:], HOPS)]
    grads = backward(rows, w, q, k, v, att, probs)
    arrived, grads = lax.optimization_barrier((arrived, grads))
    qg, kg, vg = grads
    line = line_sum([parts[0]] + arrived)
    across = swapped(line, "replica", 2)
    states = new_moments(rows, att, m, s)
    across, states = lax.optimization_barrier((across, states))
    new_first, new_second = states
    new_slot, kept, sent = outer(sc, line, across, anchor, slot_momentum, far_momentum)

    arrived = [swapped(new_slot, "replica", 4 * hop) for hop in HOPS]
    new_momentum = joined(sc, kept, swapped(sent, "replica", 1), "join_momentum")
    arrived, new_momentum = lax.optimization_barrier((arrived, new_momentum))
    whole = placed(sc, [new_slot] + arrived)
    new_anchor = joined(sc, whole, swapped(whole, "replica", 1), "join_anchor")
    return (qg[None], kg[None], vg[None], new_first[None], new_second[None], new_anchor, new_momentum)


def solution(mesh):
    rows = P("replica", None, "tensor")
    state = P("replica", "tensor", None, None)
    in_specs = (rows, rows, rows, P("replica", "tensor", None), state, state, state, P("tensor", None, None), P("tensor", "replica", None))
    out_specs = (rows, rows, rows, state, state, P("tensor", None, None), P("tensor", "replica", None))
    return jax.shard_map(local, mesh=mesh, in_specs=in_specs, out_specs=out_specs, check_vma=False)
```

```python
import functools
import math

import jax
import jax.numpy as jnp
from jax import lax
from jax.experimental import pallas as pl
from jax.experimental.pallas import tpu as pltpu
from jax.sharding import PartitionSpec as P

DH = 128
HALF = 512

beta_first = 0.9
beta_second = 0.95
correct_first = 0.9999734386011124
correct_second = 0.994079470779666
inner_rate = 0.01
decay_rate = 0.1
epsilon = 1e-08
outer_rate = 0.7
outer_beta = 0.9
workers = 16
score_scale = 1.0 / math.sqrt(DH)

NT = (((1,), (1,)), ((), ()))
TN = (((0,), (0,)), ((), ()))
f32, bf16 = jnp.float32, jnp.bfloat16
WHOLE = pl.BlockSpec(memory_space=pltpu.VMEM)
MIB = 1024 * 1024


def spot():
    replica, tensor = lax.axis_index("replica"), lax.axis_index("tensor")
    return replica & 1, tensor >> 1, tensor & 1, replica >> 2, (replica >> 1) & 1


def dot(a, b, dims=(((1,), (0,)), ((), ()))):
    return lax.dot_general(a, b, dims, preferred_element_type=f32)


def call(kernel, name, args, outs, scratch=(), mib=8, flops=0, exps=0):
    moved = sum(a.size * a.dtype.itemsize for a in args) + sum(
        math.prod(o.shape) * jnp.dtype(o.dtype).itemsize for o in outs
    )
    return pl.pallas_call(
        kernel,
        in_specs=[WHOLE for a in args],
        out_specs=[WHOLE] * len(outs),
        out_shape=outs,
        scratch_shapes=list(scratch),
        compiler_params=pltpu.CompilerParams(vmem_limit_bytes=mib * MIB),
        cost_estimate=pl.CostEstimate(flops=flops, bytes_accessed=moved, transcendentals=exps),
        name=name,
    )(*args)


def near(shape, dtype=bf16):
    return pltpu.VMEM(shape, dtype)


def far(shape, dtype=bf16):
    return jax.ShapeDtypeStruct(shape, dtype)


def columns_of(h):
    return slice(h * DH, (h + 1) * DH)


def forward_kernel(heads, q_ref, k_ref, v_ref, att_ref, p_ref):
    for h in range(heads):
        at = columns_of(h)
        s = dot(k_ref[:, at], q_ref[:, at], NT)
        top = jnp.max(s, axis=0, keepdims=True)
        e = jnp.exp((s - top) * score_scale)
        total = jnp.sum(e, axis=0, keepdims=True)
        p = (e * (1.0 / total)).astype(bf16)
        p_ref[h] = p
        att_ref[h] = dot(v_ref[:, at], p, TN).astype(bf16)


def forward(q, k, v):
    length, width = q.shape
    heads = width // DH
    return call(
        functools.partial(forward_kernel, heads),
        "attention_forward",
        [q, k, v],
        [near((heads, DH, length)), near((heads, length, length))],
        flops=4 * heads * length * length * DH,
        exps=heads * length * length,
    )


PIECES = ((0, 0, 2), (2, 0, 2), (-2, 0, 2), (1, 0, 2), (-1, 0, 2), (4, 0, 1), (4, 1, 1), (3, 0, 2), (-3, 0, 2))


def in_order(z, low, pieces, rows_ref):
    for ref, (ahead, first, lanes) in zip(pieces, PIECES):
        for n in range(lanes):
            lane = low if first + n == 0 else 1 - low
            start = (((z + 8 + ahead) % 8) * 2 + lane) * 32
            rows_ref[pl.ds(pl.multiple_of(start, 32), 32), :] = ref[n * 32 : n * 32 + 32, :]


CHUNK = 16


def moments(g, m, v):
    first = beta_first * m.astype(f32) + (1.0 - beta_first) * g
    second = beta_second * v.astype(f32) + (1.0 - beta_second) * g * g
    return first, second


def delta_kernel(ordered, side, *refs):
    sc = spot()
    if ordered:
        rows_ref, refs = refs[0], refs[1:]
    else:
        pieces, refs = refs[: len(PIECES)], refs[len(PIECES) :]
        rows_ref = refs[-2]
        in_order(sc[1], sc[2], pieces, rows_ref)
    att_ref, w_ref, m_ref, v_ref, a_ref, d_ref = refs[:6]
    g_ref = refs[-1]
    half = sc[0] if side else 1 - sc[0]
    cols = pl.ds(pl.multiple_of(half * HALF, HALF), HALF)
    for h in range(att_ref.shape[0]):
        g_ref[...] = dot(att_ref[h], rows_ref[:, cols])

        def chunk(i, carry):
            at = pl.ds(pl.multiple_of(i * CHUNK, CHUNK), CHUNK)
            first, second = moments(g_ref[at, :], m_ref[h, at, cols], v_ref[h, at, cols])
            t = second * (1.0 / correct_second)
            root = jnp.sqrt(t) + epsilon
            moved = (inner_rate / correct_first) * first / root
            kept = (1.0 - inner_rate * decay_rate) * w_ref[h, at, cols].astype(f32)
            d_ref[h, at, :] = (a_ref[h, at, cols].astype(f32) - kept + moved).astype(bf16)
            return carry

        lax.fori_loop(0, DH // CHUNK, chunk, 0, unroll=True)


def delta(side, rows, att, w, m, v, anchor):
    heads, _, length = att.shape
    wide = w.shape[2]
    ordered = not isinstance(rows, list)
    outs = [near((heads, DH, HALF))]
    if not ordered:
        outs.append(near((length, wide)))
    return call(
        functools.partial(delta_kernel, ordered, side),
        "delta_" + ("own" if side else "other"),
        ([rows] if ordered else rows) + [att, w, m, v, anchor],
        outs,
        [pltpu.VMEM((DH, HALF), f32)],
        flops=2 * heads * DH * length * HALF,
        exps=2 * heads * DH * HALF,
    )


def moments_kernel(rows_ref, att_ref, m_ref, v_ref, mo_ref, vo_ref, g_ref):
    for h in range(att_ref.shape[0]):
        g_ref[...] = dot(att_ref[h], rows_ref[...])

        def chunk(i, carry):
            at = pl.ds(pl.multiple_of(i * CHUNK, CHUNK), CHUNK)
            first, second = moments(g_ref[at, :], m_ref[h, at, :], v_ref[h, at, :])
            mo_ref[h, at, :] = first.astype(bf16)
            vo_ref[h, at, :] = second.astype(bf16)
            return carry

        lax.fori_loop(0, DH // CHUNK, chunk, 0, unroll=True)


def new_moments(rows, att, m, v):
    heads, _, length = att.shape
    wide = rows.shape[1]
    return call(
        moments_kernel,
        "moments",
        [rows, att, m, v],
        [far(m.shape), far(v.shape)],
        [pltpu.VMEM((DH, wide), f32)],
        flops=2 * heads * DH * length * wide,
    )


def backward_kernel(rows_ref, w_ref, q_ref, k_ref, v_ref, att_ref, p_ref, qg_ref, kg_ref, vg_ref):
    for h in range(att_ref.shape[0]):
        at = columns_of(h)
        grads = dot(rows_ref[...], w_ref[h], NT).astype(bf16)
        p = p_ref[h]
        turned = jnp.transpose(grads.astype(f32))
        row_dot = jnp.sum(turned * att_ref[h].astype(f32), axis=0, keepdims=True)
        vg_ref[:, at] = dot(p, grads).astype(bf16)
        grad_probs = dot(v_ref[:, at], grads, NT)
        grad_scores = (p.astype(f32) * (grad_probs - row_dot)).astype(bf16)
        kg_ref[:, at] = (dot(grad_scores, q_ref[:, at]) * score_scale).astype(bf16)
        qg = dot(k_ref[:, at], grad_scores, TN) * score_scale
        qg_ref[:, at] = jnp.transpose(qg).astype(bf16)


def backward(rows, w, q, k, v, att, p):
    length, width = q.shape
    wide = rows.shape[1]
    return call(
        backward_kernel,
        "attention_backward",
        [rows, w, q, k, v, att, p],
        [far((length, width))] * 3,
        flops=2 * length * width * wide + 8 * width * length * length,
    )


def half_of(index):
    return pl.ds(pl.multiple_of(index * HALF, HALF), HALF)


def slot_of(index):
    return pl.ds(pl.multiple_of(index * 32, 32), 32)


def load_kernel(*refs):
    count = len(refs) // 2
    sems = refs[-1]
    copies = [
        pltpu.make_async_copy(refs[n], refs[count + n], sems.at[n]) for n in range(count)
    ]
    for copy in copies:
        copy.start()
    for copy in copies:
        copy.wait()


def loaded(args):
    return pl.pallas_call(
        load_kernel,
        in_specs=[pl.BlockSpec(memory_space=pltpu.HBM)] * len(args),
        out_specs=[WHOLE] * len(args),
        out_shape=[near(a.shape, a.dtype) for a in args],
        scratch_shapes=[pltpu.SemaphoreType.DMA((len(args),))],
        compiler_params=pltpu.CompilerParams(vmem_limit_bytes=57_000_000),
        cost_estimate=pl.CostEstimate(flops=0, bytes_accessed=16 * MIB, transcendentals=0),
        name="load",
    )(*args)


def pair_kernel(a_ref, b_ref, o_ref):
    o_ref[:32, :] = a_ref[...]
    o_ref[32:, :] = b_ref[...]


def pair_of(own, other):
    rows, wide = own.shape
    return call(pair_kernel, "row_pair", [own, other], [near((2 * rows, wide))], mib=2)[0]


def share_kernel(m_ref, mine_ref, theirs_ref):
    sc = spot()
    mine_ref[...] = m_ref[:, :, half_of(sc[0])]
    theirs_ref[...] = m_ref[:, :, half_of(1 - sc[0])]


def momentum_shares(momentum):
    heads, rows, _ = momentum.shape
    shape = (heads, rows, HALF)
    return call(share_kernel, "momentum_shares", [momentum], [near(shape, f32)] * 2, mib=2)


def stack_kernel(mine_ref, came_ref, o_ref, low_ref):
    sc = spot()
    o_ref[:, pl.ds(pl.multiple_of(sc[0] * 8, 8), 8), :] = mine_ref[...]
    o_ref[:, pl.ds(pl.multiple_of((1 - sc[0]) * 8, 8), 8), :] = came_ref[...]
    low_ref[...] = o_ref[...].astype(bf16)


def momentum_stack(mine, came):
    heads, rows, _ = mine.shape
    shape = (heads, 2 * rows, HALF)
    return call(stack_kernel, "momentum_stack", [mine, came], [near(shape, f32), near(shape)], mib=2)


HOPS = (1, 3, 2)


def chip_kernel(a_ref, b_ref, *outs):
    sc = spot()
    for out, hop in zip(outs, (0,) + HOPS):
        at = slot_of(sc[3] ^ hop)
        out[...] = (a_ref[:, at, :].astype(f32) + b_ref[:, at, :].astype(f32)).astype(bf16)


def chip_sum(own, came):
    heads = own.shape[0]
    return call(chip_kernel, "chip_sum", [own, came], [near((heads, 32, HALF))] * 4, mib=2)


def line_kernel(a_ref, b_ref, c_ref, d_ref, o_ref):
    total = a_ref[...].astype(f32) + b_ref[...].astype(f32)
    o_ref[...] = (total + c_ref[...].astype(f32) + d_ref[...].astype(f32)).astype(bf16)


def line_sum(parts):
    return call(line_kernel, "line_sum", list(parts), [near(parts[0].shape)], mib=2)[0]


def outer_kernel(p_ref, q_ref, a_ref, mom_ref, low_ref, far_ref, new_ref, kept_ref, sent_ref, all_ref, avg_ref):
    sc = spot()
    y = sc[4]
    here = pl.ds(pl.multiple_of(y * 16, 16), 16)
    all_ref[:, here, :] = low_ref[...].astype(f32)
    all_ref[:, pl.ds(pl.multiple_of((1 - y) * 16, 16), 16), :] = far_ref[...].astype(f32)
    average = (p_ref[...].astype(f32) + q_ref[...].astype(f32)) * (1.0 / workers)
    avg_ref[...] = average
    momentum = outer_beta * all_ref[...] + average
    anchor = a_ref[:, slot_of(sc[3]), half_of(sc[0])].astype(f32)
    new_ref[...] = (anchor - outer_rate * (average + outer_beta * momentum)).astype(bf16)
    all_ref[:, here, :] = outer_beta * mom_ref[...] + avg_ref[:, here, :]
    kept_ref[...] = all_ref[:, pl.ds(pl.multiple_of(y * 16 + sc[0] * 8, 8), 8), :]
    sent_ref[...] = all_ref[:, pl.ds(pl.multiple_of(y * 16 + (1 - sc[0]) * 8, 8), 8), :]


def outer(p, q, anchor, momentum, low, far_low):
    heads = p.shape[0]
    row = (heads, 8, HALF)
    return call(
        outer_kernel,
        "outer_step",
        [p, q, anchor, momentum, low, far_low],
        [near(p.shape), near(row, f32), near(row, f32)],
        [pltpu.VMEM(p.shape, f32)] * 2,
        mib=4,
    )


def slots_kernel(*refs):
    sc = spot()
    for ref, hop in zip(refs[:4], (0,) + HOPS):
        refs[4][:, slot_of(sc[3] ^ hop), :] = ref[...]


def slots(parts):
    heads = parts[0].shape[0]
    return call(slots_kernel, "slots", list(parts), [near((heads, 128, HALF))], mib=2)[0]


def place_kernel(side, *refs):
    sc = spot()
    part, out, sem = refs[-3:]
    half = sc[0] if side else 1 - sc[0]
    copy = pltpu.make_async_copy(part, out.at[:, :, half_of(half)], sem)
    copy.start()
    copy.wait()


def placed(side, part, name, before=None):
    heads, rows, _ = part.shape
    args = [part] if before is None else [before, part]
    return pl.pallas_call(
        functools.partial(place_kernel, side),
        in_specs=[pl.BlockSpec(memory_space=pl.ANY)] * (len(args) - 1) + [WHOLE],
        out_specs=pl.BlockSpec(memory_space=pltpu.HBM),
        out_shape=jax.ShapeDtypeStruct((heads, rows, 2 * HALF), bf16),
        scratch_shapes=[pltpu.SemaphoreType.DMA],
        input_output_aliases={} if before is None else {0: 0},
        compiler_params=pltpu.CompilerParams(vmem_limit_bytes=2 * MIB),
        cost_estimate=pl.CostEstimate(flops=0, bytes_accessed=2 * MIB, transcendentals=0),
        name=name,
    )(*args)


def join_kernel(mine_ref, came_ref, o_ref):
    sc = spot()
    o_ref[:, :, half_of(sc[0])] = mine_ref[...]
    o_ref[:, :, half_of(1 - sc[0])] = came_ref[...]


def joined(mine, came, name):
    heads, rows, _ = mine.shape
    return call(join_kernel, name, [mine, came], [far((heads, rows, 2 * HALF), mine.dtype)], mib=2)[0]


def swapped(value, axis, bit):
    return lax.ppermute(value, axis, [(i, i ^ bit) for i in range(16)])


def from_ahead(value, k):
    return lax.ppermute(
        value, "tensor", [(i, ((i // 2 - k) % 8) * 2 + i % 2) for i in range(16)]
    )


def gather_rows(pair, opposite):
    b2 = from_ahead(pair, 2)
    m2 = from_ahead(pair, -2)
    b1 = from_ahead(pair, 1)
    m1 = from_ahead(pair, -1)
    beside = swapped(opposite, "tensor", 1)
    b3 = from_ahead(b2, 1)
    m3 = from_ahead(m2, -1)
    return [pair, b2, m2, b1, m1, opposite, beside, b3, m3]


def local(queries, key_rows, value_rows, out_grads, inner_weights, adam_first, adam_second, anchor, momentum):
    own = out_grads[0]
    other = swapped(own, "tensor", 1)
    opposite = from_ahead(own, 4)
    q, k, v, w, m, s, anchor, momentum, own = loaded(
        [queries[0], key_rows[0], value_rows[0], inner_weights[0], adam_first[0], adam_second[0], anchor, momentum, own]
    )
    mine, theirs = momentum_shares(momentum)
    near_share = swapped(theirs, "replica", 1)

    pieces = gather_rows(pair_of(own, other), opposite)
    att, probs = forward(q, k, v)

    d_other, rows = delta(0, pieces, att, w, m, s, anchor)
    came = swapped(d_other, "replica", 1)
    (d_own,) = delta(1, rows, att, w, m, s, anchor)
    came, d_own, near_share = lax.optimization_barrier((came, d_own, near_share))
    slot_momentum, low_momentum = momentum_stack(mine, near_share)
    far_momentum = swapped(low_momentum, "replica", 2)
    parts = chip_sum(d_own, came)
    arrived = [swapped(part, "replica", 4 * hop) for part, hop in zip(parts[1:], HOPS)]
    grads = backward(rows, w, q, k, v, att, probs)
    arrived, grads = lax.optimization_barrier((arrived, grads))
    qg, kg, vg = grads
    line = line_sum([parts[0]] + arrived)
    across = swapped(line, "replica", 2)
    states = new_moments(rows, att, m, s)
    across, states = lax.optimization_barrier((across, states))
    new_first, new_second = states
    new_slot, kept, sent = outer(line, across, anchor, slot_momentum, low_momentum, far_momentum)

    arrived = [swapped(new_slot, "replica", 4 * hop) for hop in HOPS]
    new_momentum = joined(kept, swapped(sent, "replica", 1), "join_momentum")
    arrived, new_momentum = lax.optimization_barrier((arrived, new_momentum))
    whole = slots([new_slot] + arrived)
    other = swapped(whole, "replica", 1)
    new_anchor = placed(1, whole, "place_own")
    other, new_anchor = lax.optimization_barrier((other, new_anchor))
    new_anchor = placed(0, other, "place_other", new_anchor)
    return (qg[None], kg[None], vg[None], new_first[None], new_second[None], new_anchor, new_momentum)


def solution(mesh):
    rows = P("replica", None, "tensor")
    state = P("replica", "tensor", None, None)
    in_specs = (rows, rows, rows, P("replica", "tensor", None), state, state, state, P("tensor", None, None), P("tensor", "replica", None))
    out_specs = (rows, rows, rows, state, state, P("tensor", None, None), P("tensor", "replica", None))
    return jax.shard_map(local, mesh=mesh, in_specs=in_specs, out_specs=out_specs, check_vma=False)
```

```python
import functools
import math

import jax
import jax.numpy as jnp
from jax import lax
from jax.experimental import pallas as pl
from jax.experimental.pallas import tpu as pltpu
from jax.sharding import PartitionSpec as P

DH = 128
HALF = 512

beta_first = 0.9
beta_second = 0.95
correct_first = 0.9999734386011124
correct_second = 0.994079470779666
inner_rate = 0.01
decay_rate = 0.1
epsilon = 1e-08
outer_rate = 0.7
outer_beta = 0.9
workers = 16
score_scale = 1.0 / math.sqrt(DH)

NT = (((1,), (1,)), ((), ()))
TN = (((0,), (0,)), ((), ()))
f32, bf16 = jnp.float32, jnp.bfloat16
WHOLE = pl.BlockSpec(memory_space=pltpu.VMEM)
MIB = 1024 * 1024


def spot():
    replica, tensor = lax.axis_index("replica"), lax.axis_index("tensor")
    return replica & 1, tensor >> 1, tensor & 1, replica >> 2, (replica >> 1) & 1


def dot(a, b, dims=(((1,), (0,)), ((), ()))):
    return lax.dot_general(a, b, dims, preferred_element_type=f32)


def call(kernel, name, args, outs, scratch=(), mib=8, flops=0, exps=0, light=False):
    moved = sum(a.size * a.dtype.itemsize for a in args) + sum(
        math.prod(o.shape) * jnp.dtype(o.dtype).itemsize for o in outs
    )
    if light:
        moved = 1024
    return pl.pallas_call(
        kernel,
        in_specs=[WHOLE for a in args],
        out_specs=[WHOLE] * len(outs),
        out_shape=outs,
        scratch_shapes=list(scratch),
        compiler_params=pltpu.CompilerParams(vmem_limit_bytes=mib * MIB),
        cost_estimate=pl.CostEstimate(flops=flops, bytes_accessed=moved, transcendentals=exps),
        name=name,
    )(*args)


def near(shape, dtype=bf16):
    return pltpu.VMEM(shape, dtype)


def far(shape, dtype=bf16):
    return jax.ShapeDtypeStruct(shape, dtype)


def columns_of(h):
    return slice(h * DH, (h + 1) * DH)


def forward_kernel(heads, q_ref, k_ref, v_ref, att_ref, p_ref):
    for h in range(heads):
        at = columns_of(h)
        s = dot(k_ref[:, at], q_ref[:, at], NT)
        top = jnp.max(s, axis=0, keepdims=True)
        e = jnp.exp((s - top) * score_scale)
        total = jnp.sum(e, axis=0, keepdims=True)
        p = (e * (1.0 / total)).astype(bf16)
        p_ref[h] = p
        att_ref[h] = dot(v_ref[:, at], p, TN).astype(bf16)


def forward(q, k, v):
    length, width = q.shape
    heads = width // DH
    return call(
        functools.partial(forward_kernel, heads),
        "attention_forward",
        [q, k, v],
        [near((heads, DH, length)), near((heads, length, length))],
        light=True,
    )


PIECES = ((0, 0, 2), (2, 0, 2), (-2, 0, 2), (1, 0, 2), (-1, 0, 2), (4, 0, 1), (4, 1, 1), (3, 0, 2), (-3, 0, 2))


def in_order(z, low, pieces, rows_ref):
    for ref, (ahead, first, lanes) in zip(pieces, PIECES):
        for n in range(lanes):
            lane = low if first + n == 0 else 1 - low
            start = (((z + 8 + ahead) % 8) * 2 + lane) * 32
            rows_ref[pl.ds(pl.multiple_of(start, 32), 32), :] = ref[n * 32 : n * 32 + 32, :]


CHUNK = 16


def moments(g, m, v):
    first = beta_first * m.astype(f32) + (1.0 - beta_first) * g
    second = beta_second * v.astype(f32) + (1.0 - beta_second) * g * g
    return first, second


def delta_kernel(ordered, side, *refs):
    sc = spot()
    if ordered:
        rows_ref, refs = refs[0], refs[1:]
    else:
        pieces, refs = refs[: len(PIECES)], refs[len(PIECES) :]
        rows_ref = refs[-2]
        in_order(sc[1], sc[2], pieces, rows_ref)
    att_ref, w_ref, m_ref, v_ref, a_ref, d_ref = refs[:6]
    g_ref = refs[-1]
    half = sc[0] if side else 1 - sc[0]
    cols = pl.ds(pl.multiple_of(half * HALF, HALF), HALF)
    for h in range(att_ref.shape[0]):
        g_ref[...] = dot(att_ref[h], rows_ref[:, cols])

        def chunk(i, carry):
            at = pl.ds(pl.multiple_of(i * CHUNK, CHUNK), CHUNK)
            first, second = moments(g_ref[at, :], m_ref[h, at, cols], v_ref[h, at, cols])
            t = second * (1.0 / correct_second)
            root = t * lax.rsqrt(t) + epsilon
            moved = (inner_rate / correct_first) * first / root
            kept = (1.0 - inner_rate * decay_rate) * w_ref[h, at, cols].astype(f32)
            d_ref[h, at, :] = (a_ref[h, at, cols].astype(f32) - kept + moved).astype(bf16)
            return carry

        lax.fori_loop(0, DH // CHUNK, chunk, 0, unroll=True)


def delta(side, rows, att, w, m, v, anchor):
    heads, _, length = att.shape
    wide = w.shape[2]
    ordered = not isinstance(rows, list)
    outs = [near((heads, DH, HALF))]
    if not ordered:
        outs.append(near((length, wide)))
    return call(
        functools.partial(delta_kernel, ordered, side),
        "delta_" + ("own" if side else "other"),
        ([rows] if ordered else rows) + [att, w, m, v, anchor],
        outs,
        [pltpu.VMEM((DH, HALF), f32)],
        flops=2 * heads * DH * length * HALF,
        exps=2 * heads * DH * HALF,
    )


def moments_kernel(rows_ref, att_ref, m_ref, v_ref, mo_ref, vo_ref, g_ref):
    for h in range(att_ref.shape[0]):
        g_ref[...] = dot(att_ref[h], rows_ref[...])

        def chunk(i, carry):
            at = pl.ds(pl.multiple_of(i * CHUNK, CHUNK), CHUNK)
            first, second = moments(g_ref[at, :], m_ref[h, at, :], v_ref[h, at, :])
            mo_ref[h, at, :] = first.astype(bf16)
            vo_ref[h, at, :] = second.astype(bf16)
            return carry

        lax.fori_loop(0, DH // CHUNK, chunk, 0, unroll=True)


def new_moments(rows, att, m, v):
    heads, _, length = att.shape
    wide = rows.shape[1]
    return call(
        moments_kernel,
        "moments",
        [rows, att, m, v],
        [far(m.shape), far(v.shape)],
        [pltpu.VMEM((DH, wide), f32)],
        flops=2 * heads * DH * length * wide,
    )


def backward_kernel(rows_ref, w_ref, q_ref, k_ref, v_ref, att_ref, p_ref, qg_ref, kg_ref, vg_ref):
    for h in range(att_ref.shape[0]):
        at = columns_of(h)
        grads = dot(rows_ref[...], w_ref[h], NT).astype(bf16)
        p = p_ref[h]
        turned = jnp.transpose(grads.astype(f32))
        row_dot = jnp.sum(turned * att_ref[h].astype(f32), axis=0, keepdims=True)
        vg_ref[:, at] = dot(p, grads).astype(bf16)
        grad_probs = dot(v_ref[:, at], grads, NT)
        grad_scores = (p.astype(f32) * (grad_probs - row_dot)).astype(bf16)
        kg_ref[:, at] = (dot(grad_scores, q_ref[:, at]) * score_scale).astype(bf16)
        qg = dot(k_ref[:, at], grad_scores, TN) * score_scale
        qg_ref[:, at] = jnp.transpose(qg).astype(bf16)


def backward(rows, w, q, k, v, att, p):
    length, width = q.shape
    wide = rows.shape[1]
    return call(
        backward_kernel,
        "attention_backward",
        [rows, w, q, k, v, att, p],
        [far((length, width))] * 3,
        flops=2 * length * width * wide + 8 * width * length * length,
    )


def half_of(index):
    return pl.ds(pl.multiple_of(index * HALF, HALF), HALF)


def slot_of(index):
    return pl.ds(pl.multiple_of(index * 32, 32), 32)


def load_kernel(*refs):
    count = len(refs) // 2
    sems = refs[-1]
    copies = [
        pltpu.make_async_copy(refs[n], refs[count + n], sems.at[n]) for n in range(count)
    ]
    for copy in copies:
        copy.start()
    for copy in copies:
        copy.wait()


def loaded(args):
    return pl.pallas_call(
        load_kernel,
        in_specs=[pl.BlockSpec(memory_space=pltpu.HBM)] * len(args),
        out_specs=[WHOLE] * len(args),
        out_shape=[near(a.shape, a.dtype) for a in args],
        scratch_shapes=[pltpu.SemaphoreType.DMA((len(args),))],
        compiler_params=pltpu.CompilerParams(vmem_limit_bytes=57_000_000),
        cost_estimate=pl.CostEstimate(flops=0, bytes_accessed=16 * MIB, transcendentals=0),
        name="load",
    )(*args)


def pair_kernel(a_ref, b_ref, o_ref):
    o_ref[:32, :] = a_ref[...]
    o_ref[32:, :] = b_ref[...]


def pair_of(own, other):
    rows, wide = own.shape
    return call(pair_kernel, "row_pair", [own, other], [near((2 * rows, wide))], mib=2)[0]


def share_kernel(m_ref, mine_ref, theirs_ref):
    sc = spot()
    mine_ref[...] = m_ref[:, :, half_of(sc[0])]
    theirs_ref[...] = m_ref[:, :, half_of(1 - sc[0])]


def momentum_shares(momentum):
    heads, rows, _ = momentum.shape
    shape = (heads, rows, HALF)
    return call(share_kernel, "momentum_shares", [momentum], [near(shape, f32)] * 2, mib=2)


def stack_kernel(mine_ref, came_ref, o_ref, low_ref):
    sc = spot()
    o_ref[:, pl.ds(pl.multiple_of(sc[0] * 8, 8), 8), :] = mine_ref[...]
    o_ref[:, pl.ds(pl.multiple_of((1 - sc[0]) * 8, 8), 8), :] = came_ref[...]
    low_ref[...] = o_ref[...].astype(bf16)


def momentum_stack(mine, came):
    heads, rows, _ = mine.shape
    shape = (heads, 2 * rows, HALF)
    return call(stack_kernel, "momentum_stack", [mine, came], [near(shape, f32), near(shape)], mib=2)


HOPS = (1, 3, 2)


def chip_kernel(a_ref, b_ref, *outs):
    sc = spot()
    for out, hop in zip(outs, (0,) + HOPS):
        at = slot_of(sc[3] ^ hop)
        out[...] = (a_ref[:, at, :].astype(f32) + b_ref[:, at, :].astype(f32)).astype(bf16)


def chip_sum(own, came):
    heads = own.shape[0]
    return call(chip_kernel, "chip_sum", [own, came], [near((heads, 32, HALF))] * 4, mib=2)


def line_kernel(a_ref, b_ref, c_ref, d_ref, o_ref):
    total = a_ref[...].astype(f32) + b_ref[...].astype(f32)
    o_ref[...] = (total + c_ref[...].astype(f32) + d_ref[...].astype(f32)).astype(bf16)


def line_sum(parts):
    return call(line_kernel, "line_sum", list(parts), [near(parts[0].shape)], mib=2)[0]


def outer_kernel(p_ref, q_ref, a_ref, mom_ref, low_ref, far_ref, new_ref, kept_ref, sent_ref, all_ref, avg_ref):
    sc = spot()
    y = sc[4]
    here = pl.ds(pl.multiple_of(y * 16, 16), 16)
    all_ref[:, here, :] = low_ref[...].astype(f32)
    all_ref[:, pl.ds(pl.multiple_of((1 - y) * 16, 16), 16), :] = far_ref[...].astype(f32)
    average = (p_ref[...].astype(f32) + q_ref[...].astype(f32)) * (1.0 / workers)
    avg_ref[...] = average
    momentum = outer_beta * all_ref[...] + average
    anchor = a_ref[:, slot_of(sc[3]), half_of(sc[0])].astype(f32)
    new_ref[...] = (anchor - outer_rate * (average + outer_beta * momentum)).astype(bf16)
    all_ref[:, here, :] = outer_beta * mom_ref[...] + avg_ref[:, here, :]
    kept_ref[...] = all_ref[:, pl.ds(pl.multiple_of(y * 16 + sc[0] * 8, 8), 8), :]
    sent_ref[...] = all_ref[:, pl.ds(pl.multiple_of(y * 16 + (1 - sc[0]) * 8, 8), 8), :]


def outer(p, q, anchor, momentum, low, far_low):
    heads = p.shape[0]
    row = (heads, 8, HALF)
    return call(
        outer_kernel,
        "outer_step",
        [p, q, anchor, momentum, low, far_low],
        [near(p.shape), near(row, f32), near(row, f32)],
        [pltpu.VMEM(p.shape, f32)] * 2,
        mib=4,
    )


def slots_kernel(*refs):
    sc = spot()
    for ref, hop in zip(refs[:4], (0,) + HOPS):
        refs[4][:, slot_of(sc[3] ^ hop), :] = ref[...]


def slots(parts):
    heads = parts[0].shape[0]
    return call(slots_kernel, "slots", list(parts), [near((heads, 128, HALF))], mib=2)[0]


def place_kernel(side, *refs):
    sc = spot()
    part, out, sem = refs[-3:]
    half = sc[0] if side else 1 - sc[0]
    copy = pltpu.make_async_copy(part, out.at[:, :, half_of(half)], sem)
    copy.start()
    copy.wait()


def placed(side, part, name, before=None):
    heads, rows, _ = part.shape
    args = [part] if before is None else [before, part]
    return pl.pallas_call(
        functools.partial(place_kernel, side),
        in_specs=[pl.BlockSpec(memory_space=pl.ANY)] * (len(args) - 1) + [WHOLE],
        out_specs=pl.BlockSpec(memory_space=pltpu.HBM),
        out_shape=jax.ShapeDtypeStruct((heads, rows, 2 * HALF), bf16),
        scratch_shapes=[pltpu.SemaphoreType.DMA],
        input_output_aliases={} if before is None else {0: 0},
        compiler_params=pltpu.CompilerParams(vmem_limit_bytes=2 * MIB),
        cost_estimate=pl.CostEstimate(flops=0, bytes_accessed=2 * MIB, transcendentals=0),
        name=name,
    )(*args)


def join_kernel(mine_ref, came_ref, o_ref):
    sc = spot()
    o_ref[:, :, half_of(sc[0])] = mine_ref[...]
    o_ref[:, :, half_of(1 - sc[0])] = came_ref[...]


def joined(mine, came, name):
    heads, rows, _ = mine.shape
    return call(join_kernel, name, [mine, came], [far((heads, rows, 2 * HALF), mine.dtype)], mib=2)[0]


def swapped(value, axis, bit):
    return lax.ppermute(value, axis, [(i, i ^ bit) for i in range(16)])


def from_ahead(value, k):
    return lax.ppermute(
        value, "tensor", [(i, ((i // 2 - k) % 8) * 2 + i % 2) for i in range(16)]
    )


def gather_rows(pair, opposite):
    b2 = from_ahead(pair, 2)
    m2 = from_ahead(pair, -2)
    b1 = from_ahead(pair, 1)
    m1 = from_ahead(pair, -1)
    beside = swapped(opposite, "tensor", 1)
    b3 = from_ahead(b2, 1)
    m3 = from_ahead(m2, -1)
    return [pair, b2, m2, b1, m1, opposite, beside, b3, m3]


def local(queries, key_rows, value_rows, out_grads, inner_weights, adam_first, adam_second, anchor, momentum):
    own = out_grads[0]
    opposite = from_ahead(own, 4)
    other = swapped(own, "tensor", 1)
    q, k, v, w, m, s, anchor, momentum, own = loaded(
        [queries[0], key_rows[0], value_rows[0], inner_weights[0], adam_first[0], adam_second[0], anchor, momentum, own]
    )
    mine, theirs = momentum_shares(momentum)
    near_share = swapped(theirs, "replica", 1)
    att, probs = forward(q, k, v)
    other, opposite, att, probs = lax.optimization_barrier((other, opposite, att, probs))
    pieces = gather_rows(pair_of(own, other), opposite)

    d_other, rows = delta(0, pieces, att, w, m, s, anchor)
    came = swapped(d_other, "replica", 1)
    (d_own,) = delta(1, rows, att, w, m, s, anchor)
    came, d_own, near_share = lax.optimization_barrier((came, d_own, near_share))
    slot_momentum, low_momentum = momentum_stack(mine, near_share)
    far_momentum = swapped(low_momentum, "replica", 2)
    parts = chip_sum(d_own, came)
    arrived = [swapped(part, "replica", 4 * hop) for part, hop in zip(parts[1:], HOPS)]
    grads = backward(rows, w, q, k, v, att, probs)
    arrived, grads = lax.optimization_barrier((arrived, grads))
    qg, kg, vg = grads
    line = line_sum([parts[0]] + arrived)
    across = swapped(line, "replica", 2)
    states = new_moments(rows, att, m, s)
    across, states = lax.optimization_barrier((across, states))
    new_first, new_second = states
    new_slot, kept, sent = outer(line, across, anchor, slot_momentum, low_momentum, far_momentum)

    arrived = [swapped(new_slot, "replica", 4 * hop) for hop in HOPS]
    new_momentum = joined(kept, swapped(sent, "replica", 1), "join_momentum")
    arrived, new_momentum = lax.optimization_barrier((arrived, new_momentum))
    whole = slots([new_slot] + arrived)
    other = swapped(whole, "replica", 1)
    new_anchor = placed(1, whole, "place_own")
    other, new_anchor = lax.optimization_barrier((other, new_anchor))
    new_anchor = placed(0, other, "place_other", new_anchor)
    return (qg[None], kg[None], vg[None], new_first[None], new_second[None], new_anchor, new_momentum)


def solution(mesh):
    rows = P("replica", None, "tensor")
    state = P("replica", "tensor", None, None)
    in_specs = (rows, rows, rows, P("replica", "tensor", None), state, state, state, P("tensor", None, None), P("tensor", "replica", None))
    out_specs = (rows, rows, rows, state, state, P("tensor", None, None), P("tensor", "replica", None))
    return jax.shard_map(local, mesh=mesh, in_specs=in_specs, out_specs=out_specs, check_vma=False)
```

```python
import functools
import math

import jax
import jax.numpy as jnp
from jax import lax
from jax.experimental import pallas as pl
from jax.experimental.pallas import tpu as pltpu
from jax.sharding import PartitionSpec as P

DH = 128
HALF = 512

beta_first = 0.9
beta_second = 0.95
correct_first = 0.9999734386011124
correct_second = 0.994079470779666
inner_rate = 0.01
decay_rate = 0.1
epsilon = 1e-08
outer_rate = 0.7
outer_beta = 0.9
workers = 16
score_scale = 1.0 / math.sqrt(DH)

NT = (((1,), (1,)), ((), ()))
TN = (((0,), (0,)), ((), ()))
f32, bf16 = jnp.float32, jnp.bfloat16
WHOLE = pl.BlockSpec(memory_space=pltpu.VMEM)
MIB = 1024 * 1024


def spot():
    replica, tensor = lax.axis_index("replica"), lax.axis_index("tensor")
    return replica & 1, tensor >> 1, tensor & 1, replica >> 2, (replica >> 1) & 1


def dot(a, b, dims=(((1,), (0,)), ((), ()))):
    return lax.dot_general(a, b, dims, preferred_element_type=f32)


def call(kernel, name, args, outs, scratch=(), mib=8, flops=0, exps=0):
    moved = sum(a.size * a.dtype.itemsize for a in args) + sum(
        math.prod(o.shape) * jnp.dtype(o.dtype).itemsize for o in outs
    )
    return pl.pallas_call(
        kernel,
        in_specs=[WHOLE for a in args],
        out_specs=[WHOLE] * len(outs),
        out_shape=outs,
        scratch_shapes=list(scratch),
        compiler_params=pltpu.CompilerParams(vmem_limit_bytes=mib * MIB),
        cost_estimate=pl.CostEstimate(flops=flops, bytes_accessed=moved, transcendentals=exps),
        name=name,
    )(*args)


def near(shape, dtype=bf16):
    return pltpu.VMEM(shape, dtype)


def far(shape, dtype=bf16):
    return jax.ShapeDtypeStruct(shape, dtype)


def columns_of(h):
    return slice(h * DH, (h + 1) * DH)


def forward_kernel(heads, q_ref, k_ref, v_ref, att_ref, p_ref):
    for h in range(heads):
        at = columns_of(h)
        s = dot(k_ref[:, at], q_ref[:, at], NT)
        top = jnp.max(s, axis=0, keepdims=True)
        e = jnp.exp((s - top) * score_scale)
        total = jnp.sum(e, axis=0, keepdims=True)
        p = (e * (1.0 / total)).astype(bf16)
        p_ref[h] = p
        att_ref[h] = dot(v_ref[:, at], p, TN).astype(bf16)


def forward(q, k, v):
    length, width = q.shape
    heads = width // DH
    return call(
        functools.partial(forward_kernel, heads),
        "attention_forward",
        [q, k, v],
        [near((heads, DH, length)), near((heads, length, length))],
        flops=4 * heads * length * length * DH,
        exps=heads * length * length,
    )


PIECES = ((0, 0, 0, 0, 2), (0, 2, 0, 0, 2), (0, -2, 0, 0, 2), (1, 0, 0, 0, 2), (-1, 0, 0, 0, 2), (0, 0, 4, 0, 1), (0, 0, 4, 1, 1), (3, 0, 0, 0, 2), (-3, 0, 0, 0, 2))


def in_order(z, low, pieces, rows_ref):
    near_sign = 1 - 2 * (z & 1)
    far_sign = 1 - (z & 2)
    for ref, (nears, fars, ahead, first, lanes) in zip(pieces, PIECES):
        place = z + 8 + ahead + nears * near_sign + fars * far_sign
        for n in range(lanes):
            lane = low if first + n == 0 else 1 - low
            start = ((place & 7) * 2 + lane) * 32
            rows_ref[pl.ds(pl.multiple_of(start, 32), 32), :] = ref[n * 32 : n * 32 + 32, :]


def turn_kernel(c_ref, d_ref, a_ref, b_ref):
    z = spot()[1]
    crossed = ((z ^ (z >> 1)) & 1) == 1

    @pl.when(crossed)
    def _():
        a_ref[...] = c_ref[...]
        b_ref[...] = d_ref[...]

    @pl.when(jnp.logical_not(crossed))
    def _():
        a_ref[...] = d_ref[...]
        b_ref[...] = c_ref[...]


def turned_pair(c, d):
    return call(turn_kernel, "turn", [c, d], [near(c.shape)] * 2, mib=2)


CHUNK = 16


def moments(g, m, v):
    first = beta_first * m.astype(f32) + (1.0 - beta_first) * g
    second = beta_second * v.astype(f32) + (1.0 - beta_second) * g * g
    return first, second


def delta_kernel(ordered, side, *refs):
    sc = spot()
    if ordered:
        rows_ref, refs = refs[0], refs[1:]
    else:
        pieces, refs = refs[: len(PIECES)], refs[len(PIECES) :]
        rows_ref = refs[-2]
        in_order(sc[1], sc[2], pieces, rows_ref)
    att_ref, w_ref, m_ref, v_ref, a_ref, d_ref = refs[:6]
    g_ref = refs[-1]
    half = sc[0] if side else 1 - sc[0]
    cols = pl.ds(pl.multiple_of(half * HALF, HALF), HALF)
    for h in range(att_ref.shape[0]):
        g_ref[...] = dot(att_ref[h], rows_ref[:, cols])

        def chunk(i, carry):
            at = pl.ds(pl.multiple_of(i * CHUNK, CHUNK), CHUNK)
            first, second = moments(g_ref[at, :], m_ref[h, at, cols], v_ref[h, at, cols])
            t = second * (1.0 / correct_second)
            root = t * lax.rsqrt(t) + epsilon
            moved = (inner_rate / correct_first) * first / root
            kept = (1.0 - inner_rate * decay_rate) * w_ref[h, at, cols].astype(f32)
            d_ref[h, at, :] = (a_ref[h, at, cols].astype(f32) - kept + moved).astype(bf16)
            return carry

        lax.fori_loop(0, DH // CHUNK, chunk, 0, unroll=True)


def delta(side, rows, att, w, m, v, anchor):
    heads, _, length = att.shape
    wide = w.shape[2]
    ordered = not isinstance(rows, list)
    outs = [near((heads, DH, HALF))]
    if not ordered:
        outs.append(near((length, wide)))
    return call(
        functools.partial(delta_kernel, ordered, side),
        "delta_" + ("own" if side else "other"),
        ([rows] if ordered else rows) + [att, w, m, v, anchor],
        outs,
        [pltpu.VMEM((DH, HALF), f32)],
        flops=2 * heads * DH * length * HALF,
        exps=2 * heads * DH * HALF,
    )


def moments_kernel(rows_ref, att_ref, m_ref, v_ref, mo_ref, vo_ref, g_ref):
    for h in range(att_ref.shape[0]):
        g_ref[...] = dot(att_ref[h], rows_ref[...])

        def chunk(i, carry):
            at = pl.ds(pl.multiple_of(i * CHUNK, CHUNK), CHUNK)
            first, second = moments(g_ref[at, :], m_ref[h, at, :], v_ref[h, at, :])
            mo_ref[h, at, :] = first.astype(bf16)
            vo_ref[h, at, :] = second.astype(bf16)
            return carry

        lax.fori_loop(0, DH // CHUNK, chunk, 0, unroll=True)


def new_moments(rows, att, m, v):
    heads, _, length = att.shape
    wide = rows.shape[1]
    return call(
        moments_kernel,
        "moments",
        [rows, att, m, v],
        [far(m.shape), far(v.shape)],
        [pltpu.VMEM((DH, wide), f32)],
        flops=2 * heads * DH * length * wide,
    )


def backward_kernel(rows_ref, w_ref, q_ref, k_ref, v_ref, att_ref, p_ref, qg_ref, kg_ref, vg_ref):
    for h in range(att_ref.shape[0]):
        at = columns_of(h)
        grads = dot(rows_ref[...], w_ref[h], NT).astype(bf16)
        p = p_ref[h]
        turned = jnp.transpose(grads.astype(f32))
        row_dot = jnp.sum(turned * att_ref[h].astype(f32), axis=0, keepdims=True)
        vg_ref[:, at] = dot(p, grads).astype(bf16)
        grad_probs = dot(v_ref[:, at], grads, NT)
        grad_scores = (p.astype(f32) * (grad_probs - row_dot)).astype(bf16)
        kg_ref[:, at] = (dot(grad_scores, q_ref[:, at]) * score_scale).astype(bf16)
        qg = dot(k_ref[:, at], grad_scores, TN) * score_scale
        qg_ref[:, at] = jnp.transpose(qg).astype(bf16)


def backward(rows, w, q, k, v, att, p):
    length, width = q.shape
    wide = rows.shape[1]
    return call(
        backward_kernel,
        "attention_backward",
        [rows, w, q, k, v, att, p],
        [far((length, width))] * 3,
        flops=2 * length * width * wide + 8 * width * length * length,
    )


def half_of(index):
    return pl.ds(pl.multiple_of(index * HALF, HALF), HALF)


def slot_of(index):
    return pl.ds(pl.multiple_of(index * 32, 32), 32)


def load_kernel(*refs):
    count = len(refs) // 2
    sems = refs[-1]
    copies = [
        pltpu.make_async_copy(refs[n], refs[count + n], sems.at[n]) for n in range(count)
    ]
    for copy in copies:
        copy.start()
    for copy in copies:
        copy.wait()


def loaded(args):
    return pl.pallas_call(
        load_kernel,
        in_specs=[pl.BlockSpec(memory_space=pltpu.HBM)] * len(args),
        out_specs=[WHOLE] * len(args),
        out_shape=[near(a.shape, a.dtype) for a in args],
        scratch_shapes=[pltpu.SemaphoreType.DMA((len(args),))],
        compiler_params=pltpu.CompilerParams(vmem_limit_bytes=57_000_000),
        cost_estimate=pl.CostEstimate(flops=0, bytes_accessed=16 * MIB, transcendentals=0),
        name="load",
    )(*args)


def pair_kernel(a_ref, b_ref, o_ref):
    o_ref[:32, :] = a_ref[...]
    o_ref[32:, :] = b_ref[...]


def pair_of(own, other):
    rows, wide = own.shape
    return call(pair_kernel, "row_pair", [own, other], [near((2 * rows, wide))], mib=2)[0]


def share_kernel(m_ref, mine_ref, theirs_ref):
    sc = spot()
    mine_ref[...] = m_ref[:, :, half_of(sc[0])]
    theirs_ref[...] = m_ref[:, :, half_of(1 - sc[0])]


def momentum_shares(momentum):
    heads, rows, _ = momentum.shape
    shape = (heads, rows, HALF)
    return call(share_kernel, "momentum_shares", [momentum], [near(shape, f32)] * 2, mib=2)


def stack_kernel(mine_ref, came_ref, o_ref, low_ref):
    sc = spot()
    o_ref[:, pl.ds(pl.multiple_of(sc[0] * 8, 8), 8), :] = mine_ref[...]
    o_ref[:, pl.ds(pl.multiple_of((1 - sc[0]) * 8, 8), 8), :] = came_ref[...]
    low_ref[...] = o_ref[...].astype(bf16)


def momentum_stack(mine, came):
    heads, rows, _ = mine.shape
    shape = (heads, 2 * rows, HALF)
    return call(stack_kernel, "momentum_stack", [mine, came], [near(shape, f32), near(shape)], mib=2)


HOPS = (1, 3, 2)


def chip_kernel(a_ref, b_ref, *outs):
    sc = spot()
    for out, hop in zip(outs, (0,) + HOPS):
        at = slot_of(sc[3] ^ hop)
        out[...] = (a_ref[:, at, :].astype(f32) + b_ref[:, at, :].astype(f32)).astype(bf16)


def chip_sum(own, came):
    heads = own.shape[0]
    return call(chip_kernel, "chip_sum", [own, came], [near((heads, 32, HALF))] * 4, mib=2)


def line_kernel(a_ref, b_ref, c_ref, d_ref, o_ref):
    total = a_ref[...].astype(f32) + b_ref[...].astype(f32)
    o_ref[...] = (total + c_ref[...].astype(f32) + d_ref[...].astype(f32)).astype(bf16)


def line_sum(parts):
    return call(line_kernel, "line_sum", list(parts), [near(parts[0].shape)], mib=2)[0]


def outer_kernel(p_ref, q_ref, a_ref, mom_ref, low_ref, far_ref, new_ref, kept_ref, sent_ref, all_ref, avg_ref):
    sc = spot()
    y = sc[4]
    here = pl.ds(pl.multiple_of(y * 16, 16), 16)
    all_ref[:, here, :] = low_ref[...].astype(f32)
    all_ref[:, pl.ds(pl.multiple_of((1 - y) * 16, 16), 16), :] = far_ref[...].astype(f32)
    average = (p_ref[...].astype(f32) + q_ref[...].astype(f32)) * (1.0 / workers)
    avg_ref[...] = average
    momentum = outer_beta * all_ref[...] + average
    anchor = a_ref[:, slot_of(sc[3]), half_of(sc[0])].astype(f32)
    new_ref[...] = (anchor - outer_rate * (average + outer_beta * momentum)).astype(bf16)
    all_ref[:, here, :] = outer_beta * mom_ref[...] + avg_ref[:, here, :]
    kept_ref[...] = all_ref[:, pl.ds(pl.multiple_of(y * 16 + sc[0] * 8, 8), 8), :]
    sent_ref[...] = all_ref[:, pl.ds(pl.multiple_of(y * 16 + (1 - sc[0]) * 8, 8), 8), :]


def outer(p, q, anchor, momentum, low, far_low):
    heads = p.shape[0]
    row = (heads, 8, HALF)
    return call(
        outer_kernel,
        "outer_step",
        [p, q, anchor, momentum, low, far_low],
        [near(p.shape), near(row, f32), near(row, f32)],
        [pltpu.VMEM(p.shape, f32)] * 2,
        mib=4,
    )


def slots_kernel(*refs):
    sc = spot()
    for ref, hop in zip(refs[:4], (0,) + HOPS):
        refs[4][:, slot_of(sc[3] ^ hop), :] = ref[...]


def slots(parts):
    heads = parts[0].shape[0]
    return call(slots_kernel, "slots", list(parts), [near((heads, 128, HALF))], mib=2)[0]


def place_kernel(side, *refs):
    sc = spot()
    part, out, sem = refs[-3:]
    half = sc[0] if side else 1 - sc[0]
    copy = pltpu.make_async_copy(part, out.at[:, :, half_of(half)], sem)
    copy.start()
    copy.wait()


def placed(side, part, name, before=None):
    heads, rows, _ = part.shape
    args = [part] if before is None else [before, part]
    return pl.pallas_call(
        functools.partial(place_kernel, side),
        in_specs=[pl.BlockSpec(memory_space=pl.ANY)] * (len(args) - 1) + [WHOLE],
        out_specs=pl.BlockSpec(memory_space=pltpu.HBM),
        out_shape=jax.ShapeDtypeStruct((heads, rows, 2 * HALF), bf16),
        scratch_shapes=[pltpu.SemaphoreType.DMA],
        input_output_aliases={} if before is None else {0: 0},
        compiler_params=pltpu.CompilerParams(vmem_limit_bytes=2 * MIB),
        cost_estimate=pl.CostEstimate(flops=0, bytes_accessed=2 * MIB, transcendentals=0),
        name=name,
    )(*args)


def join_kernel(mine_ref, came_ref, o_ref):
    sc = spot()
    o_ref[:, :, half_of(sc[0])] = mine_ref[...]
    o_ref[:, :, half_of(1 - sc[0])] = came_ref[...]


def joined(mine, came, name):
    heads, rows, _ = mine.shape
    return call(join_kernel, name, [mine, came], [far((heads, rows, 2 * HALF), mine.dtype)], mib=2)[0]


def swapped(value, axis, bit):
    return lax.ppermute(value, axis, [(i, i ^ bit) for i in range(16)])


def paired(value, partner):
    return lax.ppermute(
        value, "tensor", [(i, (partner(i // 2) % 8) * 2 + i % 2) for i in range(16)]
    )


def first_near(z):
    return z ^ 1


def second_near(z):
    return ((z + 1) ^ 1) - 1


def first_far(z):
    return z ^ 2


def second_far(z):
    return ((z + 2) ^ 2) - 2


def gather_rows(pair, opposite):
    c = paired(pair, first_far)
    d = paired(pair, second_far)
    a = paired(pair, first_near)
    b = paired(pair, second_near)
    beside = swapped(opposite, "tensor", 1)
    to_first, to_second = turned_pair(c, d)
    e = paired(to_first, first_near)
    f = paired(to_second, second_near)
    return [pair, c, d, a, b, opposite, beside, e, f]


def local(queries, key_rows, value_rows, out_grads, inner_weights, adam_first, adam_second, anchor, momentum):
    own = out_grads[0]
    other = swapped(own, "tensor", 1)
    opposite = paired(own, lambda z: z + 4)
    q, k, v, w, m, s, anchor, momentum, own = loaded(
        [queries[0], key_rows[0], value_rows[0], inner_weights[0], adam_first[0], adam_second[0], anchor, momentum, own]
    )
    mine, theirs = momentum_shares(momentum)
    near_share = swapped(theirs, "replica", 1)

    pieces = gather_rows(pair_of(own, other), opposite)
    att, probs = forward(q, k, v)

    d_other, rows = delta(0, pieces, att, w, m, s, anchor)
    came = swapped(d_other, "replica", 1)
    (d_own,) = delta(1, rows, att, w, m, s, anchor)
    came, d_own, near_share = lax.optimization_barrier((came, d_own, near_share))
    slot_momentum, low_momentum = momentum_stack(mine, near_share)
    far_momentum = swapped(low_momentum, "replica", 2)
    parts = chip_sum(d_own, came)
    arrived = [swapped(part, "replica", 4 * hop) for part, hop in zip(parts[1:], HOPS)]
    grads = backward(rows, w, q, k, v, att, probs)
    arrived, grads = lax.optimization_barrier((arrived, grads))
    qg, kg, vg = grads
    line = line_sum([parts[0]] + arrived)
    across = swapped(line, "replica", 2)
    states = new_moments(rows, att, m, s)
    across, states = lax.optimization_barrier((across, states))
    new_first, new_second = states
    new_slot, kept, sent = outer(line, across, anchor, slot_momentum, low_momentum, far_momentum)

    arrived = [swapped(new_slot, "replica", 4 * hop) for hop in HOPS]
    new_momentum = joined(kept, swapped(sent, "replica", 1), "join_momentum")
    arrived, new_momentum = lax.optimization_barrier((arrived, new_momentum))
    whole = slots([new_slot] + arrived)
    other = swapped(whole, "replica", 1)
    new_anchor = placed(1, whole, "place_own")
    other, new_anchor = lax.optimization_barrier((other, new_anchor))
    new_anchor = placed(0, other, "place_other", new_anchor)
    return (qg[None], kg[None], vg[None], new_first[None], new_second[None], new_anchor, new_momentum)


def solution(mesh):
    rows = P("replica", None, "tensor")
    state = P("replica", "tensor", None, None)
    in_specs = (rows, rows, rows, P("replica", "tensor", None), state, state, state, P("tensor", None, None), P("tensor", "replica", None))
    out_specs = (rows, rows, rows, state, state, P("tensor", None, None), P("tensor", "replica", None))
    return jax.shard_map(local, mesh=mesh, in_specs=in_specs, out_specs=out_specs, check_vma=False)
```

```python
import functools
import math

import jax
import jax.numpy as jnp
from jax import lax
from jax.experimental import pallas as pl
from jax.experimental.pallas import tpu as pltpu
from jax.sharding import PartitionSpec as P

DH = 128
HALF = 512

beta_first = 0.9
beta_second = 0.95
correct_first = 0.9999734386011124
correct_second = 0.994079470779666
inner_rate = 0.01
decay_rate = 0.1
epsilon = 1e-08
outer_rate = 0.7
outer_beta = 0.9
workers = 16
score_scale = 1.0 / math.sqrt(DH)

NT = (((1,), (1,)), ((), ()))
TN = (((0,), (0,)), ((), ()))
f32, bf16 = jnp.float32, jnp.bfloat16
WHOLE = pl.BlockSpec(memory_space=pltpu.VMEM)
MIB = 1024 * 1024


def spot():
    replica, tensor = lax.axis_index("replica"), lax.axis_index("tensor")
    return replica & 1, tensor >> 1, tensor & 1, replica >> 2, (replica >> 1) & 1


def dot(a, b, dims=(((1,), (0,)), ((), ()))):
    return lax.dot_general(a, b, dims, preferred_element_type=f32)


def call(kernel, name, args, outs, scratch=(), mib=8, flops=0, exps=0):
    moved = sum(a.size * a.dtype.itemsize for a in args) + sum(
        math.prod(o.shape) * jnp.dtype(o.dtype).itemsize for o in outs
    )
    return pl.pallas_call(
        kernel,
        in_specs=[WHOLE for a in args],
        out_specs=[WHOLE] * len(outs),
        out_shape=outs,
        scratch_shapes=list(scratch),
        compiler_params=pltpu.CompilerParams(vmem_limit_bytes=mib * MIB),
        cost_estimate=pl.CostEstimate(flops=flops, bytes_accessed=moved, transcendentals=exps),
        name=name,
    )(*args)


def near(shape, dtype=bf16):
    return pltpu.VMEM(shape, dtype)


def far(shape, dtype=bf16):
    return jax.ShapeDtypeStruct(shape, dtype)


def columns_of(h):
    return slice(h * DH, (h + 1) * DH)


def forward_kernel(heads, q_ref, k_ref, v_ref, att_ref, p_ref):
    for h in range(heads):
        at = columns_of(h)
        s = dot(k_ref[:, at], q_ref[:, at], NT)
        top = jnp.max(s, axis=0, keepdims=True)
        e = jnp.exp((s - top) * score_scale)
        total = jnp.sum(e, axis=0, keepdims=True)
        p = (e * (1.0 / total)).astype(bf16)
        p_ref[h] = p
        att_ref[h] = dot(v_ref[:, at], p, TN).astype(bf16)


def forward(q, k, v):
    length, width = q.shape
    heads = width // DH
    return call(
        functools.partial(forward_kernel, heads),
        "attention_forward",
        [q, k, v],
        [near((heads, DH, length)), near((heads, length, length))],
        flops=4 * heads * length * length * DH,
        exps=heads * length * length,
    )


PIECES = ((0, 0, 0, 2), (2, 0, 0, 2), (-2, 0, 0, 2), (1, 0, 0, 2), (-1, 0, 0, 2), (4, 0, 0, 1), (4, 0, 1, 1), (0, 3, 0, 2), (0, -3, 0, 2))


def in_order(z, low, pieces, rows_ref):
    sign = 1 - 2 * (z & 1)
    for ref, (ahead, signs, first, lanes) in zip(pieces, PIECES):
        place = z + 8 + ahead + signs * sign
        for n in range(lanes):
            lane = low if first + n == 0 else 1 - low
            start = ((place & 7) * 2 + lane) * 32
            rows_ref[pl.ds(pl.multiple_of(start, 32), 32), :] = ref[n * 32 : n * 32 + 32, :]


def turn_kernel(ahead_ref, behind_ref, first_ref, second_ref):
    even = (spot()[1] & 1) == 0

    @pl.when(even)
    def _():
        first_ref[...] = behind_ref[...]
        second_ref[...] = ahead_ref[...]

    @pl.when(jnp.logical_not(even))
    def _():
        first_ref[...] = ahead_ref[...]
        second_ref[...] = behind_ref[...]


def turned_pair(ahead, behind):
    return call(turn_kernel, "turn", [ahead, behind], [near(ahead.shape)] * 2, mib=2)


CHUNK = 16


def moments(g, m, v):
    first = beta_first * m.astype(f32) + (1.0 - beta_first) * g
    second = beta_second * v.astype(f32) + (1.0 - beta_second) * g * g
    return first, second


def delta_kernel(ordered, side, *refs):
    sc = spot()
    if ordered:
        rows_ref, refs = refs[0], refs[1:]
    else:
        pieces, refs = refs[: len(PIECES)], refs[len(PIECES) :]
        rows_ref = refs[-2]
        in_order(sc[1], sc[2], pieces, rows_ref)
    att_ref, w_ref, m_ref, v_ref, a_ref, d_ref = refs[:6]
    g_ref = refs[-1]
    half = sc[0] if side else 1 - sc[0]
    cols = pl.ds(pl.multiple_of(half * HALF, HALF), HALF)
    for h in range(att_ref.shape[0]):
        g_ref[...] = dot(att_ref[h], rows_ref[:, cols])

        def chunk(i, carry):
            at = pl.ds(pl.multiple_of(i * CHUNK, CHUNK), CHUNK)
            first, second = moments(g_ref[at, :], m_ref[h, at, cols], v_ref[h, at, cols])
            t = second * (1.0 / correct_second)
            root = t * lax.rsqrt(t) + epsilon
            moved = (inner_rate / correct_first) * first / root
            kept = (1.0 - inner_rate * decay_rate) * w_ref[h, at, cols].astype(f32)
            d_ref[h, at, :] = (a_ref[h, at, cols].astype(f32) - kept + moved).astype(bf16)
            return carry

        lax.fori_loop(0, DH // CHUNK, chunk, 0, unroll=True)


def delta(side, rows, att, w, m, v, anchor):
    heads, _, length = att.shape
    wide = w.shape[2]
    ordered = not isinstance(rows, list)
    outs = [near((heads, DH, HALF))]
    if not ordered:
        outs.append(near((length, wide)))
    return call(
        functools.partial(delta_kernel, ordered, side),
        "delta_" + ("own" if side else "other"),
        ([rows] if ordered else rows) + [att, w, m, v, anchor],
        outs,
        [pltpu.VMEM((DH, HALF), f32)],
        flops=2 * heads * DH * length * HALF,
        exps=2 * heads * DH * HALF,
    )


def moments_kernel(rows_ref, att_ref, m_ref, v_ref, mo_ref, vo_ref, g_ref):
    for h in range(att_ref.shape[0]):
        g_ref[...] = dot(att_ref[h], rows_ref[...])

        def chunk(i, carry):
            at = pl.ds(pl.multiple_of(i * CHUNK, CHUNK), CHUNK)
            first, second = moments(g_ref[at, :], m_ref[h, at, :], v_ref[h, at, :])
            mo_ref[h, at, :] = first.astype(bf16)
            vo_ref[h, at, :] = second.astype(bf16)
            return carry

        lax.fori_loop(0, DH // CHUNK, chunk, 0, unroll=True)


def new_moments(rows, att, m, v):
    heads, _, length = att.shape
    wide = rows.shape[1]
    return call(
        moments_kernel,
        "moments",
        [rows, att, m, v],
        [far(m.shape), far(v.shape)],
        [pltpu.VMEM((DH, wide), f32)],
        flops=2 * heads * DH * length * wide,
    )


def backward_kernel(rows_ref, w_ref, q_ref, k_ref, v_ref, att_ref, p_ref, qg_ref, kg_ref, vg_ref):
    for h in range(att_ref.shape[0]):
        at = columns_of(h)
        grads = dot(rows_ref[...], w_ref[h], NT).astype(bf16)
        p = p_ref[h]
        turned = jnp.transpose(grads.astype(f32))
        row_dot = jnp.sum(turned * att_ref[h].astype(f32), axis=0, keepdims=True)
        vg_ref[:, at] = dot(p, grads).astype(bf16)
        grad_probs = dot(v_ref[:, at], grads, NT)
        grad_scores = (p.astype(f32) * (grad_probs - row_dot)).astype(bf16)
        kg_ref[:, at] = (dot(grad_scores, q_ref[:, at]) * score_scale).astype(bf16)
        qg = dot(k_ref[:, at], grad_scores, TN) * score_scale
        qg_ref[:, at] = jnp.transpose(qg).astype(bf16)


def backward(rows, w, q, k, v, att, p):
    length, width = q.shape
    wide = rows.shape[1]
    return call(
        backward_kernel,
        "attention_backward",
        [rows, w, q, k, v, att, p],
        [far((length, width))] * 3,
        flops=2 * length * width * wide + 8 * width * length * length,
    )


def half_of(index):
    return pl.ds(pl.multiple_of(index * HALF, HALF), HALF)


def slot_of(index):
    return pl.ds(pl.multiple_of(index * 32, 32), 32)


def load_kernel(*refs):
    count = len(refs) // 2
    sems = refs[-1]
    copies = [
        pltpu.make_async_copy(refs[n], refs[count + n], sems.at[n]) for n in range(count)
    ]
    for copy in copies:
        copy.start()
    for copy in copies:
        copy.wait()


def loaded(args):
    return pl.pallas_call(
        load_kernel,
        in_specs=[pl.BlockSpec(memory_space=pltpu.HBM)] * len(args),
        out_specs=[WHOLE] * len(args),
        out_shape=[near(a.shape, a.dtype) for a in args],
        scratch_shapes=[pltpu.SemaphoreType.DMA((len(args),))],
        compiler_params=pltpu.CompilerParams(vmem_limit_bytes=57_000_000),
        cost_estimate=pl.CostEstimate(flops=0, bytes_accessed=16 * MIB, transcendentals=0),
        name="load",
    )(*args)


def pair_kernel(a_ref, b_ref, o_ref):
    o_ref[:32, :] = a_ref[...]
    o_ref[32:, :] = b_ref[...]


def pair_of(own, other):
    rows, wide = own.shape
    return call(pair_kernel, "row_pair", [own, other], [near((2 * rows, wide))], mib=2)[0]


def share_kernel(m_ref, mine_ref, theirs_ref):
    sc = spot()
    mine_ref[...] = m_ref[:, :, half_of(sc[0])]
    theirs_ref[...] = m_ref[:, :, half_of(1 - sc[0])]


def momentum_shares(momentum):
    heads, rows, _ = momentum.shape
    shape = (heads, rows, HALF)
    return call(share_kernel, "momentum_shares", [momentum], [near(shape, f32)] * 2, mib=2)


def stack_kernel(mine_ref, came_ref, o_ref, low_ref):
    sc = spot()
    o_ref[:, pl.ds(pl.multiple_of(sc[0] * 8, 8), 8), :] = mine_ref[...]
    o_ref[:, pl.ds(pl.multiple_of((1 - sc[0]) * 8, 8), 8), :] = came_ref[...]
    low_ref[...] = o_ref[...].astype(bf16)


def momentum_stack(mine, came):
    heads, rows, _ = mine.shape
    shape = (heads, 2 * rows, HALF)
    return call(stack_kernel, "momentum_stack", [mine, came], [near(shape, f32), near(shape)], mib=2)


HOPS = (1, 3, 2)


def chip_kernel(a_ref, b_ref, *outs):
    sc = spot()
    for out, hop in zip(outs, (0,) + HOPS):
        at = slot_of(sc[3] ^ hop)
        out[...] = (a_ref[:, at, :].astype(f32) + b_ref[:, at, :].astype(f32)).astype(bf16)


def chip_sum(own, came):
    heads = own.shape[0]
    return call(chip_kernel, "chip_sum", [own, came], [near((heads, 32, HALF))] * 4, mib=2)


def line_kernel(a_ref, b_ref, c_ref, d_ref, o_ref):
    total = a_ref[...].astype(f32) + b_ref[...].astype(f32)
    o_ref[...] = (total + c_ref[...].astype(f32) + d_ref[...].astype(f32)).astype(bf16)


def line_sum(parts):
    return call(line_kernel, "line_sum", list(parts), [near(parts[0].shape)], mib=2)[0]


def outer_kernel(p_ref, q_ref, a_ref, mom_ref, low_ref, far_ref, new_ref, kept_ref, sent_ref, all_ref, avg_ref):
    sc = spot()
    y = sc[4]
    here = pl.ds(pl.multiple_of(y * 16, 16), 16)
    all_ref[:, here, :] = low_ref[...].astype(f32)
    all_ref[:, pl.ds(pl.multiple_of((1 - y) * 16, 16), 16), :] = far_ref[...].astype(f32)
    average = (p_ref[...].astype(f32) + q_ref[...].astype(f32)) * (1.0 / workers)
    avg_ref[...] = average
    momentum = outer_beta * all_ref[...] + average
    anchor = a_ref[:, slot_of(sc[3]), half_of(sc[0])].astype(f32)
    new_ref[...] = (anchor - outer_rate * (average + outer_beta * momentum)).astype(bf16)
    all_ref[:, here, :] = outer_beta * mom_ref[...] + avg_ref[:, here, :]
    kept_ref[...] = all_ref[:, pl.ds(pl.multiple_of(y * 16 + sc[0] * 8, 8), 8), :]
    sent_ref[...] = all_ref[:, pl.ds(pl.multiple_of(y * 16 + (1 - sc[0]) * 8, 8), 8), :]


def outer(p, q, anchor, momentum, low, far_low):
    heads = p.shape[0]
    row = (heads, 8, HALF)
    return call(
        outer_kernel,
        "outer_step",
        [p, q, anchor, momentum, low, far_low],
        [near(p.shape), near(row, f32), near(row, f32)],
        [pltpu.VMEM(p.shape, f32)] * 2,
        mib=4,
    )


def slots_kernel(*refs):
    sc = spot()
    for ref, hop in zip(refs[:4], (0,) + HOPS):
        refs[4][:, slot_of(sc[3] ^ hop), :] = ref[...]


def slots(parts):
    heads = parts[0].shape[0]
    return call(slots_kernel, "slots", list(parts), [near((heads, 128, HALF))], mib=2)[0]


def place_kernel(side, *refs):
    sc = spot()
    part, out, sem = refs[-3:]
    half = sc[0] if side else 1 - sc[0]
    copy = pltpu.make_async_copy(part, out.at[:, :, half_of(half)], sem)
    copy.start()
    copy.wait()


def placed(side, part, name, before=None):
    heads, rows, _ = part.shape
    args = [part] if before is None else [before, part]
    return pl.pallas_call(
        functools.partial(place_kernel, side),
        in_specs=[pl.BlockSpec(memory_space=pl.ANY)] * (len(args) - 1) + [WHOLE],
        out_specs=pl.BlockSpec(memory_space=pltpu.HBM),
        out_shape=jax.ShapeDtypeStruct((heads, rows, 2 * HALF), bf16),
        scratch_shapes=[pltpu.SemaphoreType.DMA],
        input_output_aliases={} if before is None else {0: 0},
        compiler_params=pltpu.CompilerParams(vmem_limit_bytes=2 * MIB),
        cost_estimate=pl.CostEstimate(flops=0, bytes_accessed=2 * MIB, transcendentals=0),
        name=name,
    )(*args)


def join_kernel(mine_ref, came_ref, o_ref):
    sc = spot()
    o_ref[:, :, half_of(sc[0])] = mine_ref[...]
    o_ref[:, :, half_of(1 - sc[0])] = came_ref[...]


def joined(mine, came, name):
    heads, rows, _ = mine.shape
    return call(join_kernel, name, [mine, came], [far((heads, rows, 2 * HALF), mine.dtype)], mib=2)[0]


def swapped(value, axis, bit):
    return lax.ppermute(value, axis, [(i, i ^ bit) for i in range(16)])


def paired(value, partner):
    return lax.ppermute(
        value, "tensor", [(i, (partner(i // 2) % 8) * 2 + i % 2) for i in range(16)]
    )


def first_near(z):
    return z ^ 1


def second_near(z):
    return ((z + 1) ^ 1) - 1


def gather_rows(pair, opposite):
    b2 = paired(pair, lambda z: z - 2)
    m2 = paired(pair, lambda z: z + 2)
    b1 = paired(pair, lambda z: z - 1)
    m1 = paired(pair, lambda z: z + 1)
    beside = swapped(opposite, "tensor", 1)
    to_first, to_second = turned_pair(b2, m2)
    e = paired(to_first, first_near)
    f = paired(to_second, second_near)
    return [pair, b2, m2, b1, m1, opposite, beside, e, f]


def local(queries, key_rows, value_rows, out_grads, inner_weights, adam_first, adam_second, anchor, momentum):
    own = out_grads[0]
    other = swapped(own, "tensor", 1)
    opposite = paired(own, lambda z: z + 4)
    q, k, v, w, m, s, anchor, momentum, own = loaded(
        [queries[0], key_rows[0], value_rows[0], inner_weights[0], adam_first[0], adam_second[0], anchor, momentum, own]
    )
    mine, theirs = momentum_shares(momentum)
    near_share = swapped(theirs, "replica", 1)

    pieces = gather_rows(pair_of(own, other), opposite)
    att, probs = forward(q, k, v)

    d_other, rows = delta(0, pieces, att, w, m, s, anchor)
    came = swapped(d_other, "replica", 1)
    (d_own,) = delta(1, rows, att, w, m, s, anchor)
    came, d_own, near_share = lax.optimization_barrier((came, d_own, near_share))
    slot_momentum, low_momentum = momentum_stack(mine, near_share)
    far_momentum = swapped(low_momentum, "replica", 2)
    parts = chip_sum(d_own, came)
    arrived = [swapped(part, "replica", 4 * hop) for part, hop in zip(parts[1:], HOPS)]
    grads = backward(rows, w, q, k, v, att, probs)
    arrived, grads = lax.optimization_barrier((arrived, grads))
    qg, kg, vg = grads
    line = line_sum([parts[0]] + arrived)
    across = swapped(line, "replica", 2)
    states = new_moments(rows, att, m, s)
    across, states = lax.optimization_barrier((across, states))
    new_first, new_second = states
    new_slot, kept, sent = outer(line, across, anchor, slot_momentum, low_momentum, far_momentum)

    arrived = [swapped(new_slot, "replica", 4 * hop) for hop in HOPS]
    new_momentum = joined(kept, swapped(sent, "replica", 1), "join_momentum")
    arrived, new_momentum = lax.optimization_barrier((arrived, new_momentum))
    whole = slots([new_slot] + arrived)
    other = swapped(whole, "replica", 1)
    new_anchor = placed(1, whole, "place_own")
    other, new_anchor = lax.optimization_barrier((other, new_anchor))
    new_anchor = placed(0, other, "place_other", new_anchor)
    return (qg[None], kg[None], vg[None], new_first[None], new_second[None], new_anchor, new_momentum)


def solution(mesh):
    rows = P("replica", None, "tensor")
    state = P("replica", "tensor", None, None)
    in_specs = (rows, rows, rows, P("replica", "tensor", None), state, state, state, P("tensor", None, None), P("tensor", "replica", None))
    out_specs = (rows, rows, rows, state, state, P("tensor", None, None), P("tensor", "replica", None))
    return jax.shard_map(local, mesh=mesh, in_specs=in_specs, out_specs=out_specs, check_vma=False)
```

```python
import functools
import math

import jax
import jax.numpy as jnp
from jax import lax
from jax.experimental import pallas as pl
from jax.experimental.pallas import tpu as pltpu
from jax.sharding import PartitionSpec as P

DH = 128
HALF = 512

beta_first = 0.9
beta_second = 0.95
correct_first = 0.9999734386011124
correct_second = 0.994079470779666
inner_rate = 0.01
decay_rate = 0.1
epsilon = 1e-08
outer_rate = 0.7
outer_beta = 0.9
workers = 16
score_scale = 1.0 / math.sqrt(DH)

NT = (((1,), (1,)), ((), ()))
TN = (((0,), (0,)), ((), ()))
f32, bf16 = jnp.float32, jnp.bfloat16
WHOLE = pl.BlockSpec(memory_space=pltpu.VMEM)
MIB = 1024 * 1024


def spot():
    replica, tensor = lax.axis_index("replica"), lax.axis_index("tensor")
    return replica & 1, tensor >> 1, tensor & 1, replica >> 2, (replica >> 1) & 1


def dot(a, b, dims=(((1,), (0,)), ((), ()))):
    return lax.dot_general(a, b, dims, preferred_element_type=f32)


def call(kernel, name, args, outs, scratch=(), mib=8, flops=0, exps=0):
    moved = sum(a.size * a.dtype.itemsize for a in args) + sum(
        math.prod(o.shape) * jnp.dtype(o.dtype).itemsize for o in outs
    )
    return pl.pallas_call(
        kernel,
        in_specs=[WHOLE for a in args],
        out_specs=[WHOLE] * len(outs),
        out_shape=outs,
        scratch_shapes=list(scratch),
        compiler_params=pltpu.CompilerParams(vmem_limit_bytes=mib * MIB),
        cost_estimate=pl.CostEstimate(flops=flops, bytes_accessed=moved, transcendentals=exps),
        name=name,
    )(*args)


def near(shape, dtype=bf16):
    return pltpu.VMEM(shape, dtype)


def far(shape, dtype=bf16):
    return jax.ShapeDtypeStruct(shape, dtype)


def columns_of(h):
    return slice(h * DH, (h + 1) * DH)


def forward_kernel(heads, q_ref, k_ref, v_ref, att_ref, p_ref):
    for h in range(heads):
        at = columns_of(h)
        s = dot(k_ref[:, at], q_ref[:, at], NT)
        top = jnp.max(s, axis=0, keepdims=True)
        e = jnp.exp((s - top) * score_scale)
        total = jnp.sum(e, axis=0, keepdims=True)
        p = (e * (1.0 / total)).astype(bf16)
        p_ref[h] = p
        att_ref[h] = dot(v_ref[:, at], p, TN).astype(bf16)


def forward(q, k, v):
    length, width = q.shape
    heads = width // DH
    return call(
        functools.partial(forward_kernel, heads),
        "attention_forward",
        [q, k, v],
        [near((heads, DH, length)), near((heads, length, length))],
        flops=4 * heads * length * length * DH,
        exps=heads * length * length,
    )


PIECES = ((0, 0, 0, 2), (2, 0, 0, 2), (-2, 0, 0, 2), (1, 0, 0, 2), (-1, 0, 0, 2), (4, 0, 0, 1), (4, 0, 1, 1), (0, 3, 0, 2), (0, -3, 0, 2))


def in_order(z, low, pieces, rows_ref):
    sign = 1 - 2 * (z & 1)
    for ref, (ahead, signs, first, lanes) in zip(pieces, PIECES):
        place = z + 8 + ahead + signs * sign
        for n in range(lanes):
            lane = low if first + n == 0 else 1 - low
            start = ((place & 7) * 2 + lane) * 32
            rows_ref[pl.ds(pl.multiple_of(start, 32), 32), :] = ref[n * 32 : n * 32 + 32, :]


def turn_kernel(ahead_ref, behind_ref, first_ref, second_ref):
    even = (spot()[1] & 1) == 0

    @pl.when(even)
    def _():
        first_ref[...] = behind_ref[...]
        second_ref[...] = ahead_ref[...]

    @pl.when(jnp.logical_not(even))
    def _():
        first_ref[...] = ahead_ref[...]
        second_ref[...] = behind_ref[...]


def turned_pair(ahead, behind):
    return call(turn_kernel, "turn", [ahead, behind], [near(ahead.shape)] * 2, mib=2)


CHUNK = 16


def moments(g, m, v):
    first = beta_first * m.astype(f32) + (1.0 - beta_first) * g
    second = beta_second * v.astype(f32) + (1.0 - beta_second) * g * g
    return first, second


def delta_kernel(ordered, side, *refs):
    sc = spot()
    if ordered:
        rows_ref, refs = refs[0], refs[1:]
    else:
        pieces, refs = refs[: len(PIECES)], refs[len(PIECES) :]
        rows_ref = refs[-2]
        in_order(sc[1], sc[2], pieces, rows_ref)
    att_ref, w_ref, m_ref, v_ref, a_ref = refs[:5]
    d_ref = refs[5] if ordered else refs[6]
    g_ref = refs[-1]
    half = sc[0] if side else 1 - sc[0]
    cols = pl.ds(pl.multiple_of(half * HALF, HALF), HALF)
    if not ordered:
        share = refs[5][:, :, cols]
        d_ref[:, DH:, :] = jnp.concatenate([share, jnp.zeros_like(share)], 1).astype(bf16)
    for h in range(att_ref.shape[0]):
        g_ref[...] = dot(att_ref[h], rows_ref[:, cols])

        def chunk(i, carry):
            at = pl.ds(pl.multiple_of(i * CHUNK, CHUNK), CHUNK)
            first, second = moments(g_ref[at, :], m_ref[h, at, cols], v_ref[h, at, cols])
            t = second * (1.0 / correct_second)
            root = t * lax.rsqrt(t) + epsilon
            moved = (inner_rate / correct_first) * first / root
            kept = (1.0 - inner_rate * decay_rate) * w_ref[h, at, cols].astype(f32)
            d_ref[h, at, :] = (a_ref[h, at, cols].astype(f32) - kept + moved).astype(bf16)
            return carry

        lax.fori_loop(0, DH // CHUNK, chunk, 0, unroll=True)


def delta(side, rows, att, w, m, v, anchor, *momentum):
    heads, _, length = att.shape
    wide = w.shape[2]
    ordered = not isinstance(rows, list)
    outs = [near((heads, DH + (0 if ordered else 16), HALF))]
    if not ordered:
        outs.append(near((length, wide)))
    return call(
        functools.partial(delta_kernel, ordered, side),
        "delta_" + ("own" if side else "other"),
        ([rows] if ordered else rows) + [att, w, m, v, anchor, *momentum],
        outs,
        [pltpu.VMEM((DH, HALF), f32)],
        flops=2 * heads * DH * length * HALF,
        exps=2 * heads * DH * HALF,
    )


def moments_kernel(rows_ref, att_ref, m_ref, v_ref, mo_ref, vo_ref, g_ref):
    for h in range(att_ref.shape[0]):
        g_ref[...] = dot(att_ref[h], rows_ref[...])

        def chunk(i, carry):
            at = pl.ds(pl.multiple_of(i * CHUNK, CHUNK), CHUNK)
            first, second = moments(g_ref[at, :], m_ref[h, at, :], v_ref[h, at, :])
            mo_ref[h, at, :] = first.astype(bf16)
            vo_ref[h, at, :] = second.astype(bf16)
            return carry

        lax.fori_loop(0, DH // CHUNK, chunk, 0, unroll=True)


def new_moments(rows, att, m, v):
    heads, _, length = att.shape
    wide = rows.shape[1]
    return call(
        moments_kernel,
        "moments",
        [rows, att, m, v],
        [far(m.shape), far(v.shape)],
        [pltpu.VMEM((DH, wide), f32)],
        flops=2 * heads * DH * length * wide,
    )


def backward_kernel(rows_ref, w_ref, q_ref, k_ref, v_ref, att_ref, p_ref, qg_ref, kg_ref, vg_ref):
    for h in range(att_ref.shape[0]):
        at = columns_of(h)
        grads = dot(rows_ref[...], w_ref[h], NT).astype(bf16)
        p = p_ref[h]
        turned = jnp.transpose(grads.astype(f32))
        row_dot = jnp.sum(turned * att_ref[h].astype(f32), axis=0, keepdims=True)
        vg_ref[:, at] = dot(p, grads).astype(bf16)
        grad_probs = dot(v_ref[:, at], grads, NT)
        grad_scores = (p.astype(f32) * (grad_probs - row_dot)).astype(bf16)
        kg_ref[:, at] = (dot(grad_scores, q_ref[:, at]) * score_scale).astype(bf16)
        qg = dot(k_ref[:, at], grad_scores, TN) * score_scale
        qg_ref[:, at] = jnp.transpose(qg).astype(bf16)


def backward(rows, w, q, k, v, att, p):
    length, width = q.shape
    wide = rows.shape[1]
    return call(
        backward_kernel,
        "attention_backward",
        [rows, w, q, k, v, att, p],
        [far((length, width))] * 3,
        flops=2 * length * width * wide + 8 * width * length * length,
    )


def half_of(index):
    return pl.ds(pl.multiple_of(index * HALF, HALF), HALF)


def slot_of(index):
    return pl.ds(pl.multiple_of(index * 32, 32), 32)


def load_kernel(*refs):
    count = len(refs) // 2
    sems = refs[-1]
    copies = [
        pltpu.make_async_copy(refs[n], refs[count + n], sems.at[n]) for n in range(count)
    ]
    for copy in copies:
        copy.start()
    for copy in copies:
        copy.wait()


def loaded(args):
    return pl.pallas_call(
        load_kernel,
        in_specs=[pl.BlockSpec(memory_space=pltpu.HBM)] * len(args),
        out_specs=[WHOLE] * len(args),
        out_shape=[near(a.shape, a.dtype) for a in args],
        scratch_shapes=[pltpu.SemaphoreType.DMA((len(args),))],
        compiler_params=pltpu.CompilerParams(vmem_limit_bytes=57_000_000),
        cost_estimate=pl.CostEstimate(flops=0, bytes_accessed=16 * MIB, transcendentals=0),
        name="load",
    )(*args)


def pair_kernel(a_ref, b_ref, o_ref):
    o_ref[:32, :] = a_ref[...]
    o_ref[32:, :] = b_ref[...]


def pair_of(own, other):
    rows, wide = own.shape
    return call(pair_kernel, "row_pair", [own, other], [near((2 * rows, wide))], mib=2)[0]


HOPS = (1, 3, 2)


def chip_kernel(a_ref, b_ref, *outs):
    sc = spot()
    for out, hop in zip(outs, (0,) + HOPS):
        at = slot_of(sc[3] ^ hop)
        out[...] = (a_ref[:, at, :].astype(f32) + b_ref[:, at, :].astype(f32)).astype(bf16)


def chip_sum(own, came):
    heads = own.shape[0]
    return call(chip_kernel, "chip_sum", [own, came], [near((heads, 32, HALF))] * 4, mib=2)


def line_kernel(a_ref, b_ref, c_ref, d_ref, came_ref, mom_ref, o_ref, both_ref):
    core = spot()[0]
    total = a_ref[...].astype(f32) + b_ref[...].astype(f32)
    o_ref[:, :32, :] = (total + c_ref[...].astype(f32) + d_ref[...].astype(f32)).astype(bf16)
    share = came_ref[:, DH:, :].astype(f32)
    both_ref[:, pl.ds(pl.multiple_of(core * 8, 8), 8), :] = mom_ref[:, :, half_of(core)]
    both_ref[:, pl.ds(pl.multiple_of((1 - core) * 8, 8), 8), :] = share[:, :8, :]
    o_ref[:, 32:, :] = both_ref[...].astype(bf16)


def line_sum(parts, came, momentum):
    heads, rows, wide = parts[0].shape
    return call(
        line_kernel,
        "line_sum",
        list(parts) + [came, momentum],
        [near((heads, rows + 16, wide))],
        [pltpu.VMEM((heads, 16, wide), f32)],
        mib=4,
    )[0]


def outer_kernel(p_ref, q_ref, a_ref, new_ref, kept_ref, sent_ref, all_ref, avg_ref):
    sc = spot()
    y = sc[4]
    all_ref[:, pl.ds(pl.multiple_of(y * 16, 16), 16), :] = p_ref[:, 32:, :].astype(f32)
    all_ref[:, pl.ds(pl.multiple_of((1 - y) * 16, 16), 16), :] = q_ref[:, 32:, :].astype(f32)
    average = (p_ref[:, :32, :].astype(f32) + q_ref[:, :32, :].astype(f32)) * (1.0 / workers)
    avg_ref[...] = average
    momentum = outer_beta * all_ref[...] + average
    anchor = a_ref[:, slot_of(sc[3]), half_of(sc[0])].astype(f32)
    new_ref[...] = (anchor - outer_rate * (average + outer_beta * momentum)).astype(bf16)
    kept_ref[...] = avg_ref[:, pl.ds(pl.multiple_of(y * 16 + sc[0] * 8, 8), 8), :]
    sent_ref[...] = avg_ref[:, pl.ds(pl.multiple_of(y * 16 + (1 - sc[0]) * 8, 8), 8), :]


def outer(p, q, anchor):
    heads, _, wide = p.shape
    row, slot = (heads, 8, wide), (heads, 32, wide)
    return call(
        outer_kernel,
        "outer_step",
        [p, q, anchor],
        [near(slot), near(row, f32), near(row, f32)],
        [pltpu.VMEM(slot, f32)] * 2,
        mib=4,
    )


def momentum_kernel(mine_ref, came_ref, m_ref, o_ref):
    core = spot()[0]
    for half, average in ((core, mine_ref), (1 - core, came_ref)):
        o_ref[:, :, half_of(half)] = outer_beta * m_ref[:, :, half_of(half)] + average[...]


def next_momentum(mine, came, momentum):
    return call(momentum_kernel, "next_momentum", [mine, came, momentum], [far(momentum.shape, f32)], mib=2)[0]


def slots_kernel(*refs):
    sc = spot()
    for ref, hop in zip(refs[:4], (0,) + HOPS):
        refs[4][:, slot_of(sc[3] ^ hop), :] = ref[...]


def slots(parts):
    heads = parts[0].shape[0]
    return call(slots_kernel, "slots", list(parts), [near((heads, 128, HALF))], mib=2)[0]


def place_kernel(side, *refs):
    sc = spot()
    part, out, sem = refs[-3:]
    half = sc[0] if side else 1 - sc[0]
    copy = pltpu.make_async_copy(part, out.at[:, :, half_of(half)], sem)
    copy.start()
    copy.wait()


def placed(side, part, name, before=None):
    heads, rows, _ = part.shape
    args = [part] if before is None else [before, part]
    return pl.pallas_call(
        functools.partial(place_kernel, side),
        in_specs=[pl.BlockSpec(memory_space=pl.ANY)] * (len(args) - 1) + [WHOLE],
        out_specs=pl.BlockSpec(memory_space=pltpu.HBM),
        out_shape=jax.ShapeDtypeStruct((heads, rows, 2 * HALF), bf16),
        scratch_shapes=[pltpu.SemaphoreType.DMA],
        input_output_aliases={} if before is None else {0: 0},
        compiler_params=pltpu.CompilerParams(vmem_limit_bytes=2 * MIB),
        cost_estimate=pl.CostEstimate(flops=0, bytes_accessed=2 * MIB, transcendentals=0),
        name=name,
    )(*args)


def swapped(value, axis, bit):
    return lax.ppermute(value, axis, [(i, i ^ bit) for i in range(16)])


def paired(value, partner):
    return lax.ppermute(
        value, "tensor", [(i, (partner(i // 2) % 8) * 2 + i % 2) for i in range(16)]
    )


def first_near(z):
    return z ^ 1


def second_near(z):
    return ((z + 1) ^ 1) - 1


def gather_rows(pair, opposite):
    b2 = paired(pair, lambda z: z - 2)
    m2 = paired(pair, lambda z: z + 2)
    b1 = paired(pair, lambda z: z - 1)
    m1 = paired(pair, lambda z: z + 1)
    beside = swapped(opposite, "tensor", 1)
    to_first, to_second = turned_pair(b2, m2)
    e = paired(to_first, first_near)
    f = paired(to_second, second_near)
    return [pair, b2, m2, b1, m1, opposite, beside, e, f]


def local(queries, key_rows, value_rows, out_grads, inner_weights, adam_first, adam_second, anchor, momentum):
    own = out_grads[0]
    other = swapped(own, "tensor", 1)
    opposite = paired(own, lambda z: z + 4)
    q, k, v, w, m, s, anchor, momentum, own = loaded(
        [queries[0], key_rows[0], value_rows[0], inner_weights[0], adam_first[0], adam_second[0], anchor, momentum, own]
    )
    pieces = gather_rows(pair_of(own, other), opposite)
    att, probs = forward(q, k, v)

    d_other, rows = delta(0, pieces, att, w, m, s, anchor, momentum)
    came = swapped(d_other, "replica", 1)
    (d_own,) = delta(1, rows, att, w, m, s, anchor)
    parts = chip_sum(d_own, came)
    arrived = [swapped(part, "replica", 4 * hop) for part, hop in zip(parts[1:], HOPS)]
    grads = backward(rows, w, q, k, v, att, probs)
    arrived, grads = lax.optimization_barrier((arrived, grads))
    qg, kg, vg = grads
    line = line_sum([parts[0]] + arrived, came, momentum)
    across = swapped(line, "replica", 2)
    states = new_moments(rows, att, m, s)
    across, states = lax.optimization_barrier((across, states))
    new_first, new_second = states
    new_slot, kept, sent = outer(line, across, anchor)

    arrived = [swapped(new_slot, "replica", 4 * hop) for hop in HOPS]
    new_momentum = next_momentum(kept, swapped(sent, "replica", 1), momentum)
    arrived, new_momentum = lax.optimization_barrier((arrived, new_momentum))
    whole = slots([new_slot] + arrived)
    other = swapped(whole, "replica", 1)
    new_anchor = placed(1, whole, "place_own")
    other, new_anchor = lax.optimization_barrier((other, new_anchor))
    new_anchor = placed(0, other, "place_other", new_anchor)
    return (qg[None], kg[None], vg[None], new_first[None], new_second[None], new_anchor, new_momentum)


def solution(mesh):
    rows = P("replica", None, "tensor")
    state = P("replica", "tensor", None, None)
    in_specs = (rows, rows, rows, P("replica", "tensor", None), state, state, state, P("tensor", None, None), P("tensor", "replica", None))
    out_specs = (rows, rows, rows, state, state, P("tensor", None, None), P("tensor", "replica", None))
    return jax.shard_map(local, mesh=mesh, in_specs=in_specs, out_specs=out_specs, check_vma=False)
```

```python
import functools
import math

import jax
import jax.numpy as jnp
from jax import lax
from jax.experimental import pallas as pl
from jax.experimental.pallas import tpu as pltpu
from jax.sharding import PartitionSpec as P

DH = 128
HALF = 512

beta_first = 0.9
beta_second = 0.95
correct_first = 0.9999734386011124
correct_second = 0.994079470779666
inner_rate = 0.01
decay_rate = 0.1
epsilon = 1e-08
outer_rate = 0.7
outer_beta = 0.9
workers = 16
score_scale = 1.0 / math.sqrt(DH)

NT = (((1,), (1,)), ((), ()))
TN = (((0,), (0,)), ((), ()))
f32, bf16 = jnp.float32, jnp.bfloat16
WHOLE = pl.BlockSpec(memory_space=pltpu.VMEM)
MIB = 1024 * 1024


def spot():
    replica, tensor = lax.axis_index("replica"), lax.axis_index("tensor")
    return replica & 1, tensor >> 1, tensor & 1, replica >> 2, (replica >> 1) & 1


def dot(a, b, dims=(((1,), (0,)), ((), ()))):
    return lax.dot_general(a, b, dims, preferred_element_type=f32)


def call(kernel, name, args, outs, scratch=(), mib=8, flops=0, exps=0):
    moved = sum(a.size * a.dtype.itemsize for a in args) + sum(
        math.prod(o.shape) * jnp.dtype(o.dtype).itemsize for o in outs
    )
    return pl.pallas_call(
        kernel,
        in_specs=[WHOLE for a in args],
        out_specs=[WHOLE] * len(outs),
        out_shape=outs,
        scratch_shapes=list(scratch),
        compiler_params=pltpu.CompilerParams(vmem_limit_bytes=mib * MIB),
        cost_estimate=pl.CostEstimate(flops=flops, bytes_accessed=moved, transcendentals=exps),
        name=name,
    )(*args)


def near(shape, dtype=bf16):
    return pltpu.VMEM(shape, dtype)


def far(shape, dtype=bf16):
    return jax.ShapeDtypeStruct(shape, dtype)


def columns_of(h):
    return slice(h * DH, (h + 1) * DH)


def forward_kernel(heads, q_ref, k_ref, v_ref, att_ref, p_ref):
    for h in range(heads):
        at = columns_of(h)
        s = dot(k_ref[:, at], q_ref[:, at], NT)
        top = jnp.max(s, axis=0, keepdims=True)
        e = jnp.exp((s - top) * score_scale)
        total = jnp.sum(e, axis=0, keepdims=True)
        p = (e * (1.0 / total)).astype(bf16)
        p_ref[h] = p
        att_ref[h] = dot(v_ref[:, at], p, TN).astype(bf16)


def forward(q, k, v):
    length, width = q.shape
    heads = width // DH
    return call(
        functools.partial(forward_kernel, heads),
        "attention_forward",
        [q, k, v],
        [near((heads, DH, length)), near((heads, length, length))],
        flops=4 * heads * length * length * DH,
        exps=heads * length * length,
    )


PIECES = ((0, 0, 0, 2), (2, 0, 0, 2), (-2, 0, 0, 2), (1, 0, 0, 2), (-1, 0, 0, 2), (4, 0, 0, 1), (4, 0, 1, 1), (3, 0, 0, 2), (-3, 0, 0, 2))


def in_order(z, low, pieces, rows_ref):
    sign = 1 - 2 * (z & 1)
    for ref, (ahead, signs, first, lanes) in zip(pieces, PIECES):
        place = z + 8 + ahead + signs * sign
        for n in range(lanes):
            lane = low if first + n == 0 else 1 - low
            start = ((place & 7) * 2 + lane) * 32
            rows_ref[pl.ds(pl.multiple_of(start, 32), 32), :] = ref[n * 32 : n * 32 + 32, :]


CHUNK = 16


def moments(g, m, v):
    first = beta_first * m.astype(f32) + (1.0 - beta_first) * g
    second = beta_second * v.astype(f32) + (1.0 - beta_second) * g * g
    return first, second


def delta_kernel(ordered, side, *refs):
    sc = spot()
    if ordered:
        rows_ref, refs = refs[0], refs[1:]
    else:
        pieces, refs = refs[: len(PIECES)], refs[len(PIECES) :]
        rows_ref = refs[-2]
        in_order(sc[1], sc[2], pieces, rows_ref)
    att_ref, w_ref, m_ref, v_ref, a_ref = refs[:5]
    d_ref = refs[5] if ordered else refs[6]
    g_ref = refs[-1]
    half = sc[0] if side else 1 - sc[0]
    cols = pl.ds(pl.multiple_of(half * HALF, HALF), HALF)
    if not ordered:
        share = refs[5][:, :, cols]
        d_ref[:, DH:, :] = jnp.concatenate([share, jnp.zeros_like(share)], 1).astype(bf16)
    for h in range(att_ref.shape[0]):
        g_ref[...] = dot(att_ref[h], rows_ref[:, cols])

        def chunk(i, carry):
            at = pl.ds(pl.multiple_of(i * CHUNK, CHUNK), CHUNK)
            first, second = moments(g_ref[at, :], m_ref[h, at, cols], v_ref[h, at, cols])
            t = second * (1.0 / correct_second)
            root = t * lax.rsqrt(t) + epsilon
            moved = (inner_rate / correct_first) * first / root
            kept = (1.0 - inner_rate * decay_rate) * w_ref[h, at, cols].astype(f32)
            d_ref[h, at, :] = (a_ref[h, at, cols].astype(f32) - kept + moved).astype(bf16)
            return carry

        lax.fori_loop(0, DH // CHUNK, chunk, 0, unroll=True)


def delta(side, rows, att, w, m, v, anchor, *momentum):
    heads, _, length = att.shape
    wide = w.shape[2]
    ordered = not isinstance(rows, list)
    outs = [near((heads, DH + (0 if ordered else 16), HALF))]
    if not ordered:
        outs.append(near((length, wide)))
    return call(
        functools.partial(delta_kernel, ordered, side),
        "delta_" + ("own" if side else "other"),
        ([rows] if ordered else rows) + [att, w, m, v, anchor, *momentum],
        outs,
        [pltpu.VMEM((DH, HALF), f32)],
        flops=2 * heads * DH * length * HALF,
        exps=2 * heads * DH * HALF,
    )


def moments_kernel(rows_ref, att_ref, m_ref, v_ref, mo_ref, vo_ref, g_ref):
    for h in range(att_ref.shape[0]):
        g_ref[...] = dot(att_ref[h], rows_ref[...])

        def chunk(i, carry):
            at = pl.ds(pl.multiple_of(i * CHUNK, CHUNK), CHUNK)
            first, second = moments(g_ref[at, :], m_ref[h, at, :], v_ref[h, at, :])
            mo_ref[h, at, :] = first.astype(bf16)
            vo_ref[h, at, :] = second.astype(bf16)
            return carry

        lax.fori_loop(0, DH // CHUNK, chunk, 0, unroll=True)


def new_moments(rows, att, m, v):
    heads, _, length = att.shape
    wide = rows.shape[1]
    return call(
        moments_kernel,
        "moments",
        [rows, att, m, v],
        [far(m.shape), far(v.shape)],
        [pltpu.VMEM((DH, wide), f32)],
        flops=2 * heads * DH * length * wide,
    )


def backward_kernel(rows_ref, w_ref, q_ref, k_ref, v_ref, att_ref, p_ref, qg_ref, kg_ref, vg_ref):
    for h in range(att_ref.shape[0]):
        at = columns_of(h)
        grads = dot(rows_ref[...], w_ref[h], NT).astype(bf16)
        p = p_ref[h]
        turned = jnp.transpose(grads.astype(f32))
        row_dot = jnp.sum(turned * att_ref[h].astype(f32), axis=0, keepdims=True)
        vg_ref[:, at] = dot(p, grads).astype(bf16)
        grad_probs = dot(v_ref[:, at], grads, NT)
        grad_scores = (p.astype(f32) * (grad_probs - row_dot)).astype(bf16)
        kg_ref[:, at] = (dot(grad_scores, q_ref[:, at]) * score_scale).astype(bf16)
        qg = dot(k_ref[:, at], grad_scores, TN) * score_scale
        qg_ref[:, at] = jnp.transpose(qg).astype(bf16)


def backward(rows, w, q, k, v, att, p):
    length, width = q.shape
    wide = rows.shape[1]
    return call(
        backward_kernel,
        "attention_backward",
        [rows, w, q, k, v, att, p],
        [far((length, width))] * 3,
        flops=2 * length * width * wide + 8 * width * length * length,
    )


def half_of(index):
    return pl.ds(pl.multiple_of(index * HALF, HALF), HALF)


def slot_of(index):
    return pl.ds(pl.multiple_of(index * 32, 32), 32)


def load_kernel(*refs):
    count = len(refs) // 2
    sems = refs[-1]
    copies = [
        pltpu.make_async_copy(refs[n], refs[count + n], sems.at[n]) for n in range(count)
    ]
    for copy in copies:
        copy.start()
    for copy in copies:
        copy.wait()


def loaded(args):
    return pl.pallas_call(
        load_kernel,
        in_specs=[pl.BlockSpec(memory_space=pltpu.HBM)] * len(args),
        out_specs=[WHOLE] * len(args),
        out_shape=[near(a.shape, a.dtype) for a in args],
        scratch_shapes=[pltpu.SemaphoreType.DMA((len(args),))],
        compiler_params=pltpu.CompilerParams(vmem_limit_bytes=57_000_000),
        cost_estimate=pl.CostEstimate(flops=0, bytes_accessed=16 * MIB, transcendentals=0),
        name="load",
    )(*args)


def pair_kernel(a_ref, b_ref, o_ref):
    o_ref[:32, :] = a_ref[...]
    o_ref[32:, :] = b_ref[...]


def pair_of(own, other):
    rows, wide = own.shape
    return call(pair_kernel, "row_pair", [own, other], [near((2 * rows, wide))], mib=2)[0]


HOPS = (1, 3, 2)


def chip_kernel(a_ref, b_ref, *outs):
    sc = spot()
    for out, hop in zip(outs, (0,) + HOPS):
        at = slot_of(sc[3] ^ hop)
        out[...] = (a_ref[:, at, :].astype(f32) + b_ref[:, at, :].astype(f32)).astype(bf16)


def chip_sum(own, came):
    heads = own.shape[0]
    return call(chip_kernel, "chip_sum", [own, came], [near((heads, 32, HALF))] * 4, mib=2)


def line_kernel(a_ref, b_ref, c_ref, d_ref, came_ref, mom_ref, o_ref, both_ref):
    core = spot()[0]
    total = a_ref[...].astype(f32) + b_ref[...].astype(f32)
    o_ref[:, :32, :] = (total + c_ref[...].astype(f32) + d_ref[...].astype(f32)).astype(bf16)
    share = came_ref[:, DH:, :].astype(f32)
    both_ref[:, pl.ds(pl.multiple_of(core * 8, 8), 8), :] = mom_ref[:, :, half_of(core)]
    both_ref[:, pl.ds(pl.multiple_of((1 - core) * 8, 8), 8), :] = share[:, :8, :]
    o_ref[:, 32:, :] = both_ref[...].astype(bf16)


def line_sum(parts, came, momentum):
    heads, rows, wide = parts[0].shape
    return call(
        line_kernel,
        "line_sum",
        list(parts) + [came, momentum],
        [near((heads, rows + 16, wide))],
        [pltpu.VMEM((heads, 16, wide), f32)],
        mib=4,
    )[0]


def outer_kernel(p_ref, q_ref, a_ref, new_ref, kept_ref, sent_ref, all_ref, avg_ref):
    sc = spot()
    y = sc[4]
    all_ref[:, pl.ds(pl.multiple_of(y * 16, 16), 16), :] = p_ref[:, 32:, :].astype(f32)
    all_ref[:, pl.ds(pl.multiple_of((1 - y) * 16, 16), 16), :] = q_ref[:, 32:, :].astype(f32)
    average = (p_ref[:, :32, :].astype(f32) + q_ref[:, :32, :].astype(f32)) * (1.0 / workers)
    avg_ref[...] = average
    momentum = outer_beta * all_ref[...] + average
    anchor = a_ref[:, slot_of(sc[3]), half_of(sc[0])].astype(f32)
    new_ref[...] = (anchor - outer_rate * (average + outer_beta * momentum)).astype(bf16)
    kept_ref[...] = avg_ref[:, pl.ds(pl.multiple_of(y * 16 + sc[0] * 8, 8), 8), :]
    sent_ref[...] = avg_ref[:, pl.ds(pl.multiple_of(y * 16 + (1 - sc[0]) * 8, 8), 8), :]


def outer(p, q, anchor):
    heads, _, wide = p.shape
    row, slot = (heads, 8, wide), (heads, 32, wide)
    return call(
        outer_kernel,
        "outer_step",
        [p, q, anchor],
        [near(slot), near(row, f32), near(row, f32)],
        [pltpu.VMEM(slot, f32)] * 2,
        mib=4,
    )


def momentum_kernel(mine_ref, came_ref, m_ref, o_ref):
    core = spot()[0]
    for half, average in ((core, mine_ref), (1 - core, came_ref)):
        o_ref[:, :, half_of(half)] = outer_beta * m_ref[:, :, half_of(half)] + average[...]


def next_momentum(mine, came, momentum):
    return call(momentum_kernel, "next_momentum", [mine, came, momentum], [far(momentum.shape, f32)], mib=2)[0]


def slots_kernel(*refs):
    sc = spot()
    for ref, hop in zip(refs[:4], (0,) + HOPS):
        refs[4][:, slot_of(sc[3] ^ hop), :] = ref[...]


def slots(parts):
    heads = parts[0].shape[0]
    return call(slots_kernel, "slots", list(parts), [near((heads, 128, HALF))], mib=2)[0]


def place_kernel(side, *refs):
    sc = spot()
    part, out, sem = refs[-3:]
    half = sc[0] if side else 1 - sc[0]
    copy = pltpu.make_async_copy(part, out.at[:, :, half_of(half)], sem)
    copy.start()
    copy.wait()


def placed(side, part, name, before=None):
    heads, rows, _ = part.shape
    args = [part] if before is None else [before, part]
    return pl.pallas_call(
        functools.partial(place_kernel, side),
        in_specs=[pl.BlockSpec(memory_space=pl.ANY)] * (len(args) - 1) + [WHOLE],
        out_specs=pl.BlockSpec(memory_space=pltpu.HBM),
        out_shape=jax.ShapeDtypeStruct((heads, rows, 2 * HALF), bf16),
        scratch_shapes=[pltpu.SemaphoreType.DMA],
        input_output_aliases={} if before is None else {0: 0},
        compiler_params=pltpu.CompilerParams(vmem_limit_bytes=2 * MIB),
        cost_estimate=pl.CostEstimate(flops=0, bytes_accessed=2 * MIB, transcendentals=0),
        name=name,
    )(*args)


def swapped(value, axis, bit):
    return lax.ppermute(value, axis, [(i, i ^ bit) for i in range(16)])


def paired(value, partner):
    return lax.ppermute(
        value, "tensor", [(i, (partner(i // 2) % 8) * 2 + i % 2) for i in range(16)]
    )


def gather_rows(pair, opposite):
    b2 = paired(pair, lambda z: z - 2)
    m2 = paired(pair, lambda z: z + 2)
    b1 = paired(pair, lambda z: z - 1)
    m1 = paired(pair, lambda z: z + 1)
    beside = swapped(opposite, "tensor", 1)
    b3 = paired(b2, lambda z: z - 1)
    m3 = paired(m2, lambda z: z + 1)
    return [pair, b2, m2, b1, m1, opposite, beside, b3, m3]


def local(queries, key_rows, value_rows, out_grads, inner_weights, adam_first, adam_second, anchor, momentum):
    own = out_grads[0]
    other = swapped(own, "tensor", 1)
    opposite = paired(own, lambda z: z + 4)
    q, k, v, w, m, s, anchor, momentum, own = loaded(
        [queries[0], key_rows[0], value_rows[0], inner_weights[0], adam_first[0], adam_second[0], anchor, momentum, own]
    )
    pieces = gather_rows(pair_of(own, other), opposite)
    att, probs = forward(q, k, v)

    d_other, rows = delta(0, pieces, att, w, m, s, anchor, momentum)
    came = swapped(d_other, "replica", 1)
    (d_own,) = delta(1, rows, att, w, m, s, anchor)
    parts = chip_sum(d_own, came)
    arrived = [swapped(part, "replica", 4 * hop) for part, hop in zip(parts[1:], HOPS)]
    grads = backward(rows, w, q, k, v, att, probs)
    arrived, grads = lax.optimization_barrier((arrived, grads))
    qg, kg, vg = grads
    line = line_sum([parts[0]] + arrived, came, momentum)
    across = swapped(line, "replica", 2)
    states = new_moments(rows, att, m, s)
    across, states = lax.optimization_barrier((across, states))
    new_first, new_second = states
    new_slot, kept, sent = outer(line, across, anchor)

    arrived = [swapped(new_slot, "replica", 4 * hop) for hop in HOPS]
    new_momentum = next_momentum(kept, swapped(sent, "replica", 1), momentum)
    arrived, new_momentum = lax.optimization_barrier((arrived, new_momentum))
    whole = slots([new_slot] + arrived)
    other = swapped(whole, "replica", 1)
    new_anchor = placed(1, whole, "place_own")
    other, new_anchor = lax.optimization_barrier((other, new_anchor))
    new_anchor = placed(0, other, "place_other", new_anchor)
    return (qg[None], kg[None], vg[None], new_first[None], new_second[None], new_anchor, new_momentum)


def solution(mesh):
    rows = P("replica", None, "tensor")
    state = P("replica", "tensor", None, None)
    in_specs = (rows, rows, rows, P("replica", "tensor", None), state, state, state, P("tensor", None, None), P("tensor", "replica", None))
    out_specs = (rows, rows, rows, state, state, P("tensor", None, None), P("tensor", "replica", None))
    return jax.shard_map(local, mesh=mesh, in_specs=in_specs, out_specs=out_specs, check_vma=False)
```
